256 devices in a mesh: rep: 32 (over y, x, core), pre: 8 (over z).
Axes of the slice: x: 4, y: 4, z: 8, core: 2. Of those that a mesh axis runs over, the one named last changes fastest.
Arguments:
- queries: bfloat16 [4, 1024, 64, 128], P(None, 'rep', 'pre'), may hold values from -20 to 20
- newest_key_value: bfloat16 [4, 1024, 8, 256], P(None, 'rep', 'pre'), may hold values from -15 to 15
- prefix_kv: bfloat16 [8, 16384, 256], P(None, 'pre'), may hold values from -96 to 96
- suffix_pool: bfloat16 [1792, 8, 128, 256], P('rep', 'pre'), may hold values from -96 to 96
- page_table: int32 [1024, 2], P('rep'), may hold values from 0 to 55, as said below
- suffix_pages: int32 [1024], P('rep'), may hold values from 1 to 2, as said below
- arrival: int32 [1024], P('rep'), may hold values from 0 to 1023, as said below
Outputs:
- attended: bfloat16 [4, 1024, 64, 128], P(None, 'rep', 'pre')
The draws below stay inside these ranges and needn't reach their ends.
Inputs may be any that keep to these rules, and one draw needn't show every extreme that they name: Position j of the new layout holds the agent that stood at position arrival[j] of the old one; every position appears once; each replica sends exactly 16 of its agents to other replicas, at most one to any single replica. An agent's suffix holds suffix_pages whole pages of 128 tokens; the values of the 32 agents of one replica sum to 56. `page_table`: row a lists, in order, the pages of agent a in its own replica's pool; entries k >= suffix_pages[a] are unused; used entries of one replica never coincide.
All inputs are finite; a program needn't handle non-finite values.
Results may differ from the reference program's by a relative error of at most 0.0027.
Values may be sent and summed in bfloat16 or wider, within the bound.
A program may use at most 128 MiB of HBM per device.

```python
import jax
import jax.numpy as jnp
from jax import lax

QUERY_HEADS = 64
KEY_VALUE_HEADS = 8
HEAD_SIZE = 128
PAGE_TOKENS = 128
SUF_PAGES = 2
DECODE_STEPS = 4
PRE_DEV = 2048
AGENTS_PER_COPY = 32
POOL_PAGES = 56
MOVES = 16
AGENT_TOTAL = 1024
PREFIX_TOKENS = 16384
N_REP = 32
N_PRE = 8


def paging(key):
    key = jax.random.fold_in(key, 21)
    row_keys = jax.random.split(key, N_REP)

    def one_replica(row_key):
        leading_key, following_key = jax.random.split(row_key)
        doubled = jax.random.permutation(leading_key, AGENTS_PER_COPY) < POOL_PAGES - AGENTS_PER_COPY
        lengths = 1 + doubled.astype(jnp.int32)
        order = jax.random.permutation(following_key, POOL_PAGES).astype(jnp.int32)
        starts = jnp.cumsum(lengths) - lengths
        spots = (starts[:, None] + jnp.arange(SUF_PAGES, dtype=jnp.int32)[None, :]) % POOL_PAGES
        return (lengths, order[spots])
    return jax.vmap(one_replica)(row_keys)


def draw_queries(key, part):
    key = jax.random.fold_in(key, 11)
    drawn_values = jnp.clip(1.5 * jax.random.normal(key, (DECODE_STEPS, AGENT_TOTAL, QUERY_HEADS, HEAD_SIZE), jnp.float32), -9.0, 9.0)
    return drawn_values.astype(jnp.bfloat16)


def draw_prefix_kv(key, part):
    key = jax.random.fold_in(key, 12)
    leading_key, following_key = jax.random.split(key)
    key_portion = jnp.clip(jax.random.normal(leading_key, (KEY_VALUE_HEADS, PREFIX_TOKENS, HEAD_SIZE), jnp.float32), -6.0, 6.0)
    value_portion = jnp.clip(16.0 * jax.random.normal(following_key, (KEY_VALUE_HEADS, PREFIX_TOKENS, HEAD_SIZE), jnp.float32), -96.0, 96.0)
    return jnp.concatenate([key_portion, value_portion], axis=2).astype(jnp.bfloat16)


def draw_suffix_pool(key, part):
    key = jax.random.fold_in(key, 13)
    leading_key, following_key = jax.random.split(key)
    current_shape = (N_REP * POOL_PAGES, KEY_VALUE_HEADS, PAGE_TOKENS, HEAD_SIZE)
    key_portion = jnp.clip(1.6 * jax.random.normal(leading_key, current_shape, jnp.float32), -9.6, 9.6)
    value_portion = jnp.clip(16.0 * jax.random.normal(following_key, current_shape, jnp.float32), -96.0, 96.0)
    return jnp.concatenate([key_portion, value_portion], axis=3).astype(jnp.bfloat16)


def draw_page_table(key, part):
    lengths, table = paging(key)
    return table.reshape(AGENT_TOTAL, SUF_PAGES).astype(jnp.int32)


def draw_suffix_pages(key, part):
    lengths, table = paging(key)
    return lengths.reshape(AGENT_TOTAL).astype(jnp.int32)


def draw_arrival(key, part):
    key = jax.random.fold_in(key, 16)
    leading_key, following_key, third_key = jax.random.split(key, 3)
    moving = jax.random.permutation(leading_key, AGENTS_PER_COPY)[:MOVES]
    half_way = N_REP // 2
    others = 1 + jax.random.permutation(following_key, N_REP - 2).astype(jnp.int32)
    others = others + (others >= half_way).astype(jnp.int32)
    offsets = jnp.concatenate([jnp.full((1,), half_way, jnp.int32), others[:MOVES - 1]])
    shifting = jnp.zeros((AGENTS_PER_COPY,), jnp.int32).at[moving].set(offsets.astype(jnp.int32))
    shuffles = jax.vmap(lambda row_key: jax.random.permutation(row_key, AGENTS_PER_COPY))(jax.random.split(third_key, N_REP))
    targets = jnp.arange(N_REP, dtype=jnp.int32)[:, None]
    anchor = (targets - shifting[None, :]) % N_REP
    old_slot = shuffles[anchor, jnp.arange(AGENTS_PER_COPY)[None, :]]
    return (anchor * AGENTS_PER_COPY + old_slot).reshape(AGENT_TOTAL).astype(jnp.int32)


def block_scale(stream_key, shape, pieces, low, largest):
    def one(position, shards_of):
        steps = jax.random.uniform(jax.random.fold_in(jax.random.fold_in(stream_key, 6), position), (shards_of,), jnp.float32, low / len(pieces), largest / len(pieces))
        return jnp.repeat(jnp.exp(steps), shape[position] // shards_of).reshape((-1,) + (1,) * (len(shape) - position - 1))

    factor_of = one(*pieces[0])
    for cut in pieces[1:]:
        factor_of = factor_of * one(*cut)
    return factor_of


def bell_draw(key, shape, width, reach, cuts=(), held_as=jnp.bfloat16):
    drawn = width * jax.random.normal(key, shape, jnp.float32)
    if cuts:
        drawn = drawn * block_scale(key, shape, cuts, -0.22, 0.18)
    return jnp.clip(drawn, -reach, reach).astype(held_as)


def setup_inputs(seed: int = 0) -> dict:
    arg_keys = jax.random.split(jax.random.key(seed), 8)
    return {
        "queries": draw_queries(jax.random.fold_in(arg_keys[7], 71), 0),
        "newest_key_value": bell_draw(arg_keys[1], (DECODE_STEPS, AGENT_TOTAL, KEY_VALUE_HEADS, 2 * HEAD_SIZE), 2.5, 15.0, ((1, 32), (2, 8))),
        "prefix_kv": draw_prefix_kv(jax.random.fold_in(arg_keys[7], 71), 0),
        "suffix_pool": draw_suffix_pool(jax.random.fold_in(arg_keys[7], 71), 0),
        "page_table": draw_page_table(jax.random.fold_in(arg_keys[7], 71), 0),
        "suffix_pages": draw_suffix_pages(jax.random.fold_in(arg_keys[7], 71), 0),
        "arrival": draw_arrival(jax.random.fold_in(arg_keys[7], 71), 0),
    }


negative_fill = -1.0e30


def prefix_partial(block_of_queries, shard_kv, score_scale):
    grouping_size = QUERY_HEADS // KEY_VALUE_HEADS
    raised_values = block_of_queries.astype(jnp.float32).reshape(DECODE_STEPS, AGENTS_PER_COPY, KEY_VALUE_HEADS, grouping_size, HEAD_SIZE)
    key_portion = shard_kv[:, :, :HEAD_SIZE].astype(jnp.float32)
    value_portion = shard_kv[:, :, HEAD_SIZE:].astype(jnp.float32)
    scores = jnp.einsum("sahgd,hkd->sahgk", raised_values, key_portion, precision=lax.Precision.HIGHEST) * score_scale
    peak_score = jnp.max(scores, axis=-1)
    weights = jnp.exp(scores - peak_score[..., None])
    weight_sum = jnp.sum(weights, axis=-1)
    rounded = lax.optimization_barrier(weights.astype(jnp.bfloat16)).astype(jnp.float32)
    partial_value = jnp.einsum("sahgk,hkd->sahgd", rounded, value_portion, precision=lax.Precision.HIGHEST) / weight_sum[..., None]
    log_total = peak_score + jnp.log(weight_sum)
    return partial_value.reshape(DECODE_STEPS, AGENTS_PER_COPY, QUERY_HEADS, HEAD_SIZE), log_total.reshape(DECODE_STEPS, AGENTS_PER_COPY, QUERY_HEADS)


def suffix_partial(block_of_queries, cache_of_suffix, fresh_block, lengths, score_scale):
    grouping_size = QUERY_HEADS // KEY_VALUE_HEADS
    tokens_in_cache = SUF_PAGES * PAGE_TOKENS
    cached_entries = cache_of_suffix.transpose(0, 2, 1, 3, 4).reshape(AGENTS_PER_COPY, KEY_VALUE_HEADS, tokens_in_cache, 2 * HEAD_SIZE)
    recent = fresh_block.transpose(1, 2, 0, 3)
    key_values = jnp.concatenate([cached_entries, recent], axis=2).astype(jnp.float32)
    raised_values = block_of_queries.astype(jnp.float32).reshape(DECODE_STEPS, AGENTS_PER_COPY, KEY_VALUE_HEADS, grouping_size, HEAD_SIZE)
    scores = jnp.einsum("sahgd,ahkd->sahgk", raised_values, key_values[..., :HEAD_SIZE], precision=lax.Precision.HIGHEST) * score_scale
    token_ids = jnp.arange(tokens_in_cache + DECODE_STEPS, dtype=jnp.int32)
    step_ids = jnp.arange(DECODE_STEPS, dtype=jnp.int32)
    in_cache = token_ids[None, :] < (lengths.astype(jnp.int32) * PAGE_TOKENS)[:, None]
    in_fresh = (token_ids[None, :] >= tokens_in_cache) & (token_ids[None, :] - tokens_in_cache <= step_ids[:, None])
    usable = (in_cache[None, :, :] | in_fresh[:, None, :])[:, :, None, None, :]
    scores = jnp.where(usable, scores, negative_fill)
    peak_score = jnp.max(scores, axis=-1)
    weights = jnp.where(usable, jnp.exp(scores - peak_score[..., None]), 0.0)
    weight_sum = jnp.sum(weights, axis=-1)
    rounded = lax.optimization_barrier(weights.astype(jnp.bfloat16)).astype(jnp.float32)
    partial_value = jnp.einsum("sahgk,ahkd->sahgd", rounded, key_values[..., HEAD_SIZE:], precision=lax.Precision.HIGHEST) / weight_sum[..., None]
    log_total = peak_score + jnp.log(weight_sum)
    return partial_value.reshape(DECODE_STEPS, AGENTS_PER_COPY, QUERY_HEADS, HEAD_SIZE), log_total.reshape(DECODE_STEPS, AGENTS_PER_COPY, QUERY_HEADS)


def reference(queries, newest_key_value, prefix_kv, suffix_pool, page_table, suffix_pages, arrival):
    score_scale = HEAD_SIZE ** -0.5
    count_of_blocks = AGENT_TOTAL // AGENTS_PER_COPY
    query_blocks = queries.reshape(DECODE_STEPS, count_of_blocks, AGENTS_PER_COPY, QUERY_HEADS, HEAD_SIZE).transpose(1, 0, 2, 3, 4)
    newest_blocks = newest_key_value.reshape(DECODE_STEPS, count_of_blocks, AGENTS_PER_COPY, KEY_VALUE_HEADS, 2 * HEAD_SIZE).transpose(1, 0, 2, 3, 4)
    arrival_blocks = arrival.reshape(count_of_blocks, AGENTS_PER_COPY)

    def one_block(pair_item):
        block_of_queries, fresh_block, old_agents = pair_item
        old_rep = old_agents // AGENTS_PER_COPY
        pool_rows = old_rep[:, None] * POOL_PAGES + page_table[old_agents]
        cache_of_suffix = suffix_pool[pool_rows]
        suffix_out, suffix_lse = suffix_partial(block_of_queries, cache_of_suffix, fresh_block, suffix_pages[old_agents], score_scale)
        out_list = [suffix_out]
        lse_list = [suffix_lse]
        for shard_id in range(N_PRE):
            shard_kv = lax.slice_in_dim(prefix_kv, shard_id * PRE_DEV, (shard_id + 1) * PRE_DEV, axis=1)
            shard_out, shard_lse = prefix_partial(block_of_queries, shard_kv, score_scale)
            out_list.append(shard_out)
            lse_list.append(shard_lse)
        stacked_lse = jnp.stack(lse_list, 0)
        peak_lse = jnp.max(stacked_lse, axis=0)
        total_lse = peak_lse + jnp.log(jnp.sum(jnp.exp(stacked_lse - peak_lse[None]), axis=0))
        result = jnp.zeros((DECODE_STEPS, AGENTS_PER_COPY, QUERY_HEADS, HEAD_SIZE), jnp.float32)
        for set_out, set_lse in zip(out_list, lse_list):
            result = result + jnp.exp(set_lse - total_lse)[..., None] * set_out
        return result.astype(jnp.bfloat16)

    result = lax.map(one_block, (query_blocks, newest_blocks, arrival_blocks))
    return result.transpose(1, 0, 2, 3, 4).reshape(DECODE_STEPS, AGENT_TOTAL, QUERY_HEADS, HEAD_SIZE)
```

```python
import functools

import jax
import jax.numpy as jnp
from jax import lax
from jax.experimental import pallas as pl
from jax.experimental.pallas import tpu as pltpu
from jax.sharding import PartitionSpec as P

MESH = pl.DeviceIdType.MESH
BF16 = jnp.bfloat16
F32 = jnp.float32
I32 = jnp.int32

N_REP, N_PRE = 32, 8
X_SIZE, Y_SIZE = 4, 4
TOKENS = 2048
HALF = TOKENS // 2
QUARTER = HALF // 4
AGENTS = 32
ROWS = 32
HEAD = 128
PAGE = 128
POOL = 56
MSG = 64
BLOCK = 256
BLOCKS = AGENTS * ROWS // BLOCK
CHUNK = 256
TO_LOG2 = HEAD ** (-0.5) * 1.4426950408889634
LOW = -1e30


def kernel(
    local_ref, arr_row_ref, arr_col_ref, arrival_ref, table_ref, pages_ref, prefix_ref, pool_hbm,
    out_ref,
    kv, pool, asked, req_out, meta, idx_v, idx_s, res, res_lse, ans_out, ans_in,
    s0, s1, m0, m1, acc, m_run, l_run,
    zs, zr, xs, xr, ss, sr, rqs, rqr, mts, mtr, rps, rpr, loc,
):
    rep = lax.axis_index("rep")
    pre = lax.axis_index("pre")
    core = lax.rem(rep, 2)
    x = lax.rem(rep // 2, X_SIZE)
    y = rep // (2 * X_SIZE)
    sibling = rep + 1 - 2 * core

    def at_xy(xx, yy):
        return (lax.rem(yy + Y_SIZE, Y_SIZE) * X_SIZE + lax.rem(xx + X_SIZE, X_SIZE)) * 2 + core

    x_up, x_down = at_xy(x + 1, y), at_xy(x - 1, y)
    y_up, y_down = at_xy(x, y + 1), at_xy(x, y - 1)
    mine = lax.rem(x + 2 * y, 4)

    def spot(which, size=QUARTER, extra=0):
        start = core * HALF + lax.rem(which + 4, 4) * QUARTER + extra
        return pl.ds(pl.multiple_of(start, 128), size)

    def shard_of(k):
        far = (k + 1) // 2
        return lax.rem(pre + jnp.where(lax.rem(k, 2) == 1, far, -far) + N_PRE, N_PRE)

    def z_send(plane):
        where = spot(mine)
        return pltpu.make_async_remote_copy(
            src_ref=prefix_ref.at[plane, where, :], dst_ref=kv.at[pre, where, :],
            send_sem=zs.at[plane], recv_sem=zr.at[pre], device_id=(rep, plane), device_id_type=MESH)

    def z_recv(p):
        where = spot(mine)
        return pltpu.make_async_remote_copy(
            src_ref=kv.at[p, where, :], dst_ref=kv.at[p, where, :],
            send_sem=zs.at[p], recv_sem=zr.at[p], device_id=(rep, p), device_id_type=MESH)

    def xy_copies(p, which, who):
        out = []
        for i, (size, extra) in enumerate(
            ((QUARTER, 0), (QUARTER, 0), (QUARTER // 2, 0), (QUARTER // 2, QUARTER // 2))
        ):
            ref = kv.at[p, spot(which[i], size, extra), :]
            out.append(pltpu.make_async_remote_copy(
                src_ref=ref, dst_ref=ref, send_sem=xs.at[p, i], recv_sem=xr.at[p, i],
                device_id=(who[i], pre), device_id_type=MESH))
        return out

    def xy_send(p):
        return xy_copies(p, (mine, mine, mine, mine), (x_up, x_down, y_up, y_down))

    def xy_recv(p):
        return xy_copies(p, (mine - 1, mine + 1, mine + 2, mine + 2), (x_down, x_up, y_down, y_up))

    def sib_copy(p, half):
        ref = kv.at[p, pl.ds(pl.multiple_of(half * HALF, HALF), HALF), :]
        return pltpu.make_async_remote_copy(
            src_ref=ref, dst_ref=ref, send_sem=ss.at[p], recv_sem=sr.at[p],
            device_id=(sibling, pre), device_id_type=MESH)

    def request(src_slot, dst_slot, other):
        return pltpu.make_async_remote_copy(
            src_ref=req_out.at[src_slot], dst_ref=asked.at[dst_slot],
            send_sem=rqs.at[src_slot], recv_sem=rqr.at[dst_slot], device_id=(other, pre), device_id_type=MESH)

    def tell(dst_slot, send_slot, other):
        return pltpu.make_async_remote_copy(
            src_ref=arr_row_ref, dst_ref=meta.at[dst_slot],
            send_sem=mts.at[send_slot], recv_sem=mtr.at[dst_slot], device_id=(other, pre), device_id_type=MESH)

    def answer(src_slot, dst_slot, other):
        return pltpu.make_async_remote_copy(
            src_ref=ans_out.at[src_slot], dst_ref=ans_in.at[dst_slot],
            send_sem=rps.at[src_slot], recv_sem=rpr.at[dst_slot], device_id=(other, pre), device_id_type=MESH)

    def peers(fn):
        def one(i, c):
            fn(lax.rem(rep + i, N_REP))
            return c
        lax.fori_loop(1, N_REP, one, 0)

    def planes(fn):
        def one(k, c):
            fn(shard_of(k))
            return c
        lax.fori_loop(1, N_PRE, one, 0)

    own = pltpu.make_async_copy(prefix_ref.at[pre], kv.at[pre], loc.at[0])
    own.start()
    pool_copy = pltpu.make_async_copy(pool_hbm, pool, loc.at[1])
    pool_copy.start()
    barrier = pltpu.get_barrier_semaphore()
    peers(lambda o: pl.semaphore_signal(barrier, inc=1, device_id=(o, pre), device_id_type=MESH))
    planes(lambda p: pl.semaphore_signal(barrier, inc=1, device_id=(rep, p), device_id_type=MESH))

    lane = lax.broadcasted_iota(I32, (AGENTS, HEAD), 1)
    sub = lax.broadcasted_iota(I32, (AGENTS, HEAD), 0)
    from_rep = lax.shift_right_logical(arr_col_ref[...], 5)
    asker = jnp.max(jnp.where(from_rep == lane, sub, 0), axis=0, keepdims=True)
    idx_v[...] = jnp.broadcast_to(asker, (8, HEAD))
    put = pltpu.make_async_copy(idx_v, idx_s, loc.at[2])
    put.start()
    put.wait()

    pl.semaphore_wait(barrier, N_REP - 1 + N_PRE - 1)
    planes(lambda p: z_send(p).start())

    def ask(o):
        tell(rep, o, o).start()
        req_out[o] = local_ref[idx_s[0, o]]
        request(o, rep, o).start()
    peers(ask)
    asked[rep] = local_ref[0]
    meta[rep] = arr_row_ref[...]
    ans_in[rep] = jnp.zeros((ROWS, 2 * HEAD), BF16)

    m_run[...] = jnp.full_like(m_run, LOW)
    l_run[...] = jnp.zeros_like(l_run)
    acc[...] = jnp.zeros_like(acc)
    score_bufs, peak_bufs = (s0, s1), (m0, m1)
    per = BLOCK // ROWS

    def block_queries(b):
        return local_ref[b * per:(b + 1) * per, :ROWS, :].reshape(BLOCK, HEAD)

    def score_chunk(q, p, u, kc, peak):
        k = kv[p, kc * CHUNK:(kc + 1) * CHUNK, :HEAD]
        s = lax.dot_general(q, k, (((1,), (1,)), ((), ())), preferred_element_type=F32)
        score_bufs[u][:, kc * CHUNK:(kc + 1) * CHUNK] = s
        for j in range(CHUNK // 128):
            part = s[:, j * 128:(j + 1) * 128]
            peak = part if peak is None else jnp.maximum(peak, part)
        return peak

    def keep_peak(u, peak):
        peak_bufs[u][...] = jnp.broadcast_to(jnp.max(peak, axis=1, keepdims=True), (BLOCK, 128))

    def step(b, p, b_next, p_next):
        u, v = b % 2, b_next % 2
        q = block_queries(b_next)
        peak = peak_bufs[u][:, :1]
        nxt = None
        total = None
        out = None
        for kc in range(TOKENS // CHUNK):
            nxt = score_chunk(q, p_next, v, kc, nxt)
            w = jnp.exp2((score_bufs[u][:, kc * CHUNK:(kc + 1) * CHUNK] - peak) * TO_LOG2)
            for j in range(CHUNK // 128):
                part = w[:, j * 128:(j + 1) * 128]
                total = part if total is None else total + part
            d = jnp.dot(w.astype(BF16), kv[p, kc * CHUNK:(kc + 1) * CHUNK, HEAD:], preferred_element_type=F32)
            out = d if out is None else out + d
        keep_peak(v, nxt)
        rows = slice(b * BLOCK, (b + 1) * BLOCK)
        total = jnp.sum(total, axis=1, keepdims=True)
        top = peak_bufs[u][...] * TO_LOG2
        old = m_run[rows, :]
        new = jnp.maximum(old, top)
        f_old, f_new = jnp.exp2(old - new), jnp.exp2(top - new)
        m_run[rows, :] = new
        l_run[rows, :] = l_run[rows, :] * f_old + total * f_new
        acc[rows, :] = acc[rows, :] * f_old + out * f_new

    def place_agents():
        peers(lambda o: tell(o, o, o).wait_recv())
        everyone = meta[:, 0, :]
        spots = sub * AGENTS + lane
        rows = []
        for a in range(AGENTS):
            hit = (everyone == rep * AGENTS + a) & (lane < AGENTS)
            rows.append(jnp.max(jnp.where(hit, spots, 0), axis=0, keepdims=True))
        table = jnp.concatenate(rows, axis=0)
        where = jnp.max(table, axis=1, keepdims=True)
        where = jnp.broadcast_to(where, (AGENTS, HEAD))
        leaver = jnp.max(jnp.where(lax.shift_right_logical(where, 5) == lane, sub, 0), axis=0, keepdims=True)
        here = jnp.max(jnp.where(lane == sub, where, 0), axis=0, keepdims=True)
        both = jnp.where(lax.broadcasted_iota(I32, (8, HEAD), 0) == 0, leaver, here)
        idx_v[...] = both
        put.start()
        put.wait()

    def suffix_one(a):
        at = idx_s[1, a]
        src = lax.shift_right_logical(at, 5)
        slot = lax.rem(at, AGENTS)
        msg = jnp.where(src == rep, local_ref[slot], asked[src])
        q, kn, vn = msg[:ROWS], msg[ROWS:ROWS + 16], msg[ROWS + 16:]
        page0, page1 = table_ref[a, 0], table_ref[a, 1]
        dims = (((1,), (1,)), ((), ()))
        c0 = lax.dot_general(q, pool[page0, :, :HEAD], dims, preferred_element_type=F32)
        c1 = lax.dot_general(q, pool[page1, :, :HEAD], dims, preferred_element_type=F32)
        cn = lax.dot_general(q, kn, dims, preferred_element_type=F32)
        c1 = jnp.where(pages_ref[a] > 1, c1, LOW)
        rows_n = lax.broadcasted_iota(I32, (ROWS, 16), 0)
        cols_n = lax.broadcasted_iota(I32, (ROWS, 16), 1)
        cn = jnp.where(cols_n <= lax.shift_right_logical(rows_n, 3), cn, LOW)
        peak = jnp.maximum(
            jnp.max(jnp.maximum(c0, c1), axis=1, keepdims=True), jnp.max(cn, axis=1, keepdims=True))
        w0 = jnp.exp2((c0 - peak) * TO_LOG2)
        w1 = jnp.exp2((c1 - peak) * TO_LOG2)
        wn = jnp.exp2((cn - peak) * TO_LOG2)
        total = jnp.sum(w0 + w1, axis=1, keepdims=True) + jnp.sum(wn, axis=1, keepdims=True)
        o = jnp.dot(w0.astype(BF16), pool[page0, :, HEAD:], preferred_element_type=F32)
        o = o + jnp.dot(w1.astype(BF16), pool[page1, :, HEAD:], preferred_element_type=F32)
        o = o + jnp.dot(wn.astype(BF16), vn, preferred_element_type=F32)
        res[a] = o / total
        res_lse[a] = jnp.broadcast_to(peak * TO_LOG2 + jnp.log2(total), (ROWS, HEAD))

    def suffix_all():
        def some(i, c):
            for j in range(4):
                suffix_one(i * 4 + j)
            return c
        lax.fori_loop(0, AGENTS // 4, some, 0)

    def send_answers():
        lanes = lax.broadcasted_iota(I32, (ROWS, HEAD), 1)

        def one(o):
            a = idx_s[0, o]
            ans_out[o, :, :HEAD] = res[a].astype(BF16)
            lse = res_lse[a]
            hi = lse.astype(BF16).astype(F32)
            mid = (lse - hi).astype(BF16).astype(F32)
            low = lse - hi - mid
            ans_out[o, :, HEAD:] = jnp.where(lanes < 32, hi, jnp.where(lanes < 64, mid, low)).astype(BF16)
            answer(o, rep, o).start()
        peers(one)

    def forward_z(p):
        z_recv(p).wait_recv()
        for c in xy_send(p):
            c.start()

    def forward_xy(p):
        for c in xy_recv(p):
            c.wait_recv()
        sib_copy(p, core).start()

    own.wait()
    peak = None
    q_first = block_queries(0)
    for kc in range(TOKENS // CHUNK):
        peak = score_chunk(q_first, pre, 0, kc, peak)
    keep_peak(0, peak)

    def shard(k, c):
        p = shard_of(k)
        p_next = shard_of(jnp.minimum(k + 1, N_PRE - 1))

        @pl.when((k >= 1) & (k + 2 < N_PRE))
        def _():
            forward_z(shard_of(k + 2))

        step(0, p, 1, p)

        @pl.when((k >= 2) & (k + 1 < N_PRE))
        def _():
            forward_xy(shard_of(k + 1))

        step(1, p, 2, p)
        step(2, p, 3, p)

        @pl.when(k == 0)
        def _():
            forward_z(shard_of(1))
            forward_z(shard_of(2))
            place_agents()
            forward_xy(shard_of(1))
            pool_copy.wait()
            peers(lambda o: request(o, o, o).wait_recv())
            suffix_all()
            forward_xy(shard_of(2))
            send_answers()

        @pl.when(k + 1 < N_PRE)
        def _():
            sib_copy(p_next, 1 - core).wait_recv()

        step(3, p, 0, p_next)
        return c

    lax.fori_loop(0, N_PRE, shard, 0)

    peers(lambda o: answer(o, o, o).wait_recv())

    def finish(i, c):
        for u in range(4):
            j = i * 4 + u
            old = arrival_ref[j]
            src = lax.shift_right_logical(old, 5)
            slot = lax.rem(old, AGENTS)
            got = ans_in[src].astype(F32)
            stays = src == rep
            part = jnp.where(stays, res[slot], got[:, :HEAD])
            lse_got = got[:, HEAD:HEAD + 1] + got[:, HEAD + 32:HEAD + 33] + got[:, HEAD + 64:HEAD + 65]
            lse = jnp.where(stays, res_lse[slot], lse_got)
            rows = pl.ds(pl.multiple_of(j * ROWS, ROWS), ROWS)
            m = m_run[rows, :]
            top = jnp.maximum(m, lse)
            f, g = jnp.exp2(m - top), jnp.exp2(lse - top)
            out_ref[j] = ((acc[rows, :] * f + part * g) / (l_run[rows, :] * f + g)).astype(BF16)
        return c

    lax.fori_loop(0, AGENTS // 4, finish, 0)

    def sent(o):
        tell(rep, o, o).wait_send()
        request(o, rep, o).wait_send()
        answer(o, rep, o).wait_send()
    peers(sent)

    def left(p):
        z_send(p).wait_send()
        for c in xy_send(p):
            c.wait_send()
        sib_copy(p, core).wait_send()
    planes(left)


def attend(local, arr_row, arr_col, arrival, page_table, suffix_pages, prefix_kv, pool):
    vmem = pl.BlockSpec(memory_space=pltpu.VMEM)
    smem = pl.BlockSpec(memory_space=pltpu.SMEM)
    hbm = pl.BlockSpec(memory_space=pl.ANY)
    dma = pltpu.SemaphoreType.DMA
    rows = AGENTS * ROWS
    return pl.pallas_call(
        kernel,
        out_shape=jax.ShapeDtypeStruct((AGENTS, ROWS, HEAD), BF16),
        in_specs=[vmem, vmem, vmem, smem, smem, smem, hbm, hbm],
        out_specs=vmem,
        scratch_shapes=[
            pltpu.VMEM((N_PRE, TOKENS, 2 * HEAD), BF16),
            pltpu.VMEM((POOL, PAGE, 2 * HEAD), BF16),
            pltpu.VMEM((N_REP, MSG, HEAD), BF16),
            pltpu.VMEM((N_REP, MSG, HEAD), BF16),
            pltpu.VMEM((N_REP, 8, HEAD), I32),
            pltpu.VMEM((8, HEAD), I32),
            pltpu.SMEM((8, HEAD), I32),
            pltpu.VMEM((AGENTS, ROWS, HEAD), F32),
            pltpu.VMEM((AGENTS, ROWS, HEAD), F32),
            pltpu.VMEM((N_REP, ROWS, 2 * HEAD), BF16),
            pltpu.VMEM((N_REP, ROWS, 2 * HEAD), BF16),
            pltpu.VMEM((BLOCK, TOKENS), F32),
            pltpu.VMEM((BLOCK, TOKENS), F32),
            pltpu.VMEM((BLOCK, 128), F32),
            pltpu.VMEM((BLOCK, 128), F32),
            pltpu.VMEM((rows, HEAD), F32),
            pltpu.VMEM((rows, HEAD), F32),
            pltpu.VMEM((rows, HEAD), F32),
            dma((N_PRE,)), dma((N_PRE,)),
            dma((N_PRE, 4)), dma((N_PRE, 4)),
            dma((N_PRE,)), dma((N_PRE,)),
            dma((N_REP,)), dma((N_REP,)),
            dma((N_REP,)), dma((N_REP,)),
            dma((N_REP,)), dma((N_REP,)),
            dma((3,)),
        ],
        compiler_params=pltpu.CompilerParams(
            collective_id=0, has_side_effects=True, vmem_limit_bytes=48 << 20),
    )(local, arr_row, arr_col, arrival, page_table, suffix_pages, prefix_kv, pool)


def per_device(queries, newest_key_value, prefix_kv, suffix_pool, page_table, suffix_pages, arrival):
    steps, agents, group, head = queries.shape
    q = queries.transpose(1, 0, 2, 3).reshape(agents, steps * group, head)
    new = newest_key_value[:, :, 0, :].transpose(1, 0, 2)
    new = jnp.pad(new, ((0, 0), (0, 16 - steps), (0, 0)))
    local = jnp.concatenate([q, new[..., :head], new[..., head:]], axis=1)
    arr_row = jnp.broadcast_to(jnp.pad(arrival, (0, head - agents), constant_values=-1)[None, :], (8, head))
    arr_col = jnp.broadcast_to(arrival[:, None], (agents, head))
    pool = suffix_pool.reshape(suffix_pool.shape[0], suffix_pool.shape[2], suffix_pool.shape[3])
    out = attend(local, arr_row, arr_col, arrival, page_table, suffix_pages, prefix_kv, pool)
    return out.reshape(agents, steps, group, head).transpose(1, 0, 2, 3)


def solution(mesh):
    return jax.shard_map(
        per_device,
        mesh=mesh,
        in_specs=(
            P(None, "rep", "pre", None),
            P(None, "rep", "pre", None),
            P(None, "pre", None),
            P("rep", "pre", None, None),
            P("rep", None),
            P("rep"),
            P("rep"),
        ),
        out_specs=P(None, "rep", "pre", None),
        check_vma=False,
    )
```

```python
import functools

import jax
import jax.numpy as jnp
from jax import lax
from jax.experimental import pallas as pl
from jax.experimental.pallas import tpu as pltpu
from jax.sharding import PartitionSpec as P

MESH = pl.DeviceIdType.MESH
BF16 = jnp.bfloat16
F32 = jnp.float32
I32 = jnp.int32

N_REP, N_PRE = 32, 8
X_SIZE, Y_SIZE = 4, 4
TOKENS = 2048
HALF = TOKENS // 2
QUARTER = HALF // 4
AGENTS = 32
ROWS = 32
HEAD = 128
PAGE = 128
POOL = 56
MSG = 48
BLOCK = 256
BLOCKS = AGENTS * ROWS // BLOCK
CHUNK = 256
TO_LOG2 = HEAD ** (-0.5) * 1.4426950408889634
LOW = -1e30


def kernel(
    q_ref, new_ref, arrival_ref, table_ref, pages_ref, prefix_ref, pool_hbm,
    out_ref,
    kv, pool, local, tail, asked, req_out, ask_v, ask_s, idx_v, idx_s, res, res_lse, ans_out, ans_in,
    s0, s1, m0, m1, acc, m_run, l_run,
    zs, zr, xs, xr, ss, sr, rqs, rqr, rps, rpr, loc,
):
    rep = lax.axis_index("rep")
    pre = lax.axis_index("pre")
    core = lax.rem(rep, 2)
    x = lax.rem(rep // 2, X_SIZE)
    y = rep // (2 * X_SIZE)
    sibling = rep + 1 - 2 * core

    def at_xy(xx, yy):
        return (lax.rem(yy + Y_SIZE, Y_SIZE) * X_SIZE + lax.rem(xx + X_SIZE, X_SIZE)) * 2 + core

    x_up, x_down = at_xy(x + 1, y), at_xy(x - 1, y)
    y_up, y_down = at_xy(x, y + 1), at_xy(x, y - 1)
    mine = lax.rem(x + 2 * y, 4)

    def spot(which, size=QUARTER, extra=0):
        start = core * HALF + lax.rem(which + 4, 4) * QUARTER + extra
        return pl.ds(pl.multiple_of(start, 128), size)

    def shard_of(k):
        far = (k + 1) // 2
        return lax.rem(pre + jnp.where(lax.rem(k, 2) == 1, far, -far) + N_PRE, N_PRE)

    def z_send(plane):
        where = spot(mine)
        return pltpu.make_async_remote_copy(
            src_ref=prefix_ref.at[plane, where, :], dst_ref=kv.at[pre, where, :],
            send_sem=zs.at[plane], recv_sem=zr.at[pre], device_id=(rep, plane), device_id_type=MESH)

    def z_recv(p):
        where = spot(mine)
        return pltpu.make_async_remote_copy(
            src_ref=kv.at[p, where, :], dst_ref=kv.at[p, where, :],
            send_sem=zs.at[p], recv_sem=zr.at[p], device_id=(rep, p), device_id_type=MESH)

    def xy_copies(p, which, who):
        out = []
        for i, (size, extra) in enumerate(
            ((QUARTER, 0), (QUARTER, 0), (QUARTER // 2, 0), (QUARTER // 2, QUARTER // 2))
        ):
            ref = kv.at[p, spot(which[i], size, extra), :]
            out.append(pltpu.make_async_remote_copy(
                src_ref=ref, dst_ref=ref, send_sem=xs.at[p], recv_sem=xr.at[p],
                device_id=(who[i], pre), device_id_type=MESH))
        return out

    def xy_send(p):
        return xy_copies(p, (mine, mine, mine, mine), (x_up, x_down, y_up, y_down))

    def xy_all(p):
        ref = kv.at[p, pl.ds(0, 3 * QUARTER), :]
        return pltpu.make_async_remote_copy(
            src_ref=ref, dst_ref=ref, send_sem=xs.at[p], recv_sem=xr.at[p],
            device_id=(x_up, pre), device_id_type=MESH)

    def sib_copy(p, half):
        ref = kv.at[p, pl.ds(pl.multiple_of(half * HALF, HALF), HALF), :]
        return pltpu.make_async_remote_copy(
            src_ref=ref, dst_ref=ref, send_sem=ss.at[p], recv_sem=sr.at[p],
            device_id=(sibling, pre), device_id_type=MESH)

    def request(slot, other):
        return pltpu.make_async_remote_copy(
            src_ref=req_out.at[slot], dst_ref=asked.at[rep],
            send_sem=rqs.at[0], recv_sem=rqr.at[0], device_id=(other, pre), device_id_type=MESH)

    def answer(slot, other):
        return pltpu.make_async_remote_copy(
            src_ref=ans_out.at[slot], dst_ref=ans_in.at[rep],
            send_sem=rps.at[0], recv_sem=rpr.at[0], device_id=(other, pre), device_id_type=MESH)

    def all_of(buf, send, recv):
        ref = buf.at[pl.ds(0, N_REP - 1)]
        return pltpu.make_async_remote_copy(
            src_ref=ref, dst_ref=ref, send_sem=send.at[0], recv_sem=recv.at[0],
            device_id=(sibling, pre), device_id_type=MESH)

    def peers(fn):
        def one(i, c):
            fn(lax.rem(rep + i, N_REP))
            return c
        lax.fori_loop(1, N_REP, one, 0)

    def planes(fn):
        def one(k, c):
            fn(shard_of(k))
            return c
        lax.fori_loop(1, N_PRE, one, 0)

    own = pltpu.make_async_copy(prefix_ref.at[pre], kv.at[pre], loc.at[0])
    own.start()
    pool_copy = pltpu.make_async_copy(pool_hbm, pool, loc.at[1])
    pool_copy.start()
    barrier = pltpu.get_barrier_semaphore()
    peers(lambda o: pl.semaphore_signal(barrier, inc=1, device_id=(o, pre), device_id_type=MESH))
    planes(lambda p: pl.semaphore_signal(barrier, inc=1, device_id=(rep, p), device_id_type=MESH))

    lane = lax.broadcasted_iota(I32, (AGENTS, HEAD), 1)
    sub = lax.broadcasted_iota(I32, (AGENTS, HEAD), 0)
    old = jnp.zeros((AGENTS, HEAD), I32)
    for j in range(AGENTS):
        old = jnp.where(sub == j, arrival_ref[j], old)
    from_rep = lax.shift_right_logical(old, 5)
    asker = jnp.max(jnp.where(from_rep == lane, sub, 0), axis=0, keepdims=True)
    ask_v[...] = jnp.broadcast_to(asker, (8, HEAD))
    ask_put = pltpu.make_async_copy(ask_v, ask_s, loc.at[2])
    ask_put.start()

    for t in range(4):
        tail[:, t, :] = new_ref[t, :, :HEAD].astype(F32)
        tail[:, 4 + t, :] = new_ref[t, :, HEAD:].astype(F32)
    tail[:, 8, :] = (old & 31).astype(F32)
    tail[:, 9, :] = from_rep.astype(F32)
    for t in range(10, 16):
        tail[:, t, :] = jnp.zeros((AGENTS, HEAD), F32)

    def build(i, c):
        for u in range(8):
            j = i * 8 + u
            rows = jnp.concatenate([q_ref[t, j].astype(F32) for t in range(4)] + [tail[j]], axis=0)
            local[j] = rows.astype(BF16)
        return c
    lax.fori_loop(0, AGENTS // 8, build, 0)

    ask_put.wait()
    pl.semaphore_wait(barrier, N_REP - 1 + N_PRE - 1)

    def z_sends(first, last):
        def one(k, c):
            z_send(shard_of(k)).start()
            return c
        lax.fori_loop(first, last, one, 0)
    z_sends(1, 5)

    def ask(o):
        req_out[o] = local[ask_s[0, o]]
        request(o, o).start()
    peers(ask)
    asked[rep] = jnp.zeros((MSG, HEAD), BF16)
    ans_in[rep] = jnp.zeros((ROWS, 2 * HEAD), BF16)

    m_run[...] = jnp.full_like(m_run, LOW)
    l_run[...] = jnp.zeros_like(l_run)
    acc[...] = jnp.zeros_like(acc)
    score_bufs, peak_bufs = (s0, s1), (m0, m1)
    per = BLOCK // ROWS

    def block_queries(b):
        return local[b * per:(b + 1) * per, :ROWS, :].reshape(BLOCK, HEAD)

    def score_chunk(q, p, u, kc, peak):
        k = kv[p, kc * CHUNK:(kc + 1) * CHUNK, :HEAD]
        s = lax.dot_general(q, k, (((1,), (1,)), ((), ())), preferred_element_type=F32)
        score_bufs[u][:, kc * CHUNK:(kc + 1) * CHUNK] = s
        for j in range(CHUNK // 128):
            part = s[:, j * 128:(j + 1) * 128]
            peak = part if peak is None else jnp.maximum(peak, part)
        return peak

    def keep_peak(u, peak):
        peak_bufs[u][...] = jnp.broadcast_to(jnp.max(peak, axis=1, keepdims=True), (BLOCK, 128))

    def step(b, p, b_next, p_next):
        u, v = b % 2, b_next % 2
        q = block_queries(b_next)
        peak = peak_bufs[u][:, :1]
        nxt = None
        total = None
        out = None
        for kc in range(TOKENS // CHUNK):
            nxt = score_chunk(q, p_next, v, kc, nxt)
            w = jnp.exp2((score_bufs[u][:, kc * CHUNK:(kc + 1) * CHUNK] - peak) * TO_LOG2)
            for j in range(CHUNK // 128):
                part = w[:, j * 128:(j + 1) * 128]
                total = part if total is None else total + part
            d = jnp.dot(w.astype(BF16), kv[p, kc * CHUNK:(kc + 1) * CHUNK, HEAD:], preferred_element_type=F32)
            out = d if out is None else out + d
        keep_peak(v, nxt)
        rows = slice(b * BLOCK, (b + 1) * BLOCK)
        total = jnp.sum(total, axis=1, keepdims=True)
        top = peak_bufs[u][...] * TO_LOG2
        old = m_run[rows, :]
        new = jnp.maximum(old, top)
        f_old, f_new = jnp.exp2(old - new), jnp.exp2(top - new)
        m_run[rows, :] = new
        l_run[rows, :] = l_run[rows, :] * f_old + total * f_new
        acc[rows, :] = acc[rows, :] * f_old + out * f_new

    def place_agents():
        all_of(asked, rqs, rqr).wait_recv()
        told = asked[:, ROWS:, :].astype(F32)
        slots = told[:, 8, :].astype(I32)
        reps = told[:, 9, :].astype(I32)
        for_me = (reps == rep) & (sub != rep)
        moved = jnp.where(for_me & (slots == lane), sub, 0)
        stays = jnp.where((from_rep == rep) & ((old & 31) == lane), sub + AGENTS, 0)
        at = jnp.max(jnp.maximum(moved, stays), axis=0, keepdims=True)
        idx_v[:AGENTS, :] = jnp.where(for_me, slots & 31, 0)
        idx_v[AGENTS:, :] = jnp.broadcast_to(at, (8, HEAD))
        put = pltpu.make_async_copy(idx_v, idx_s, loc.at[2])
        put.start()
        put.wait()

    dims = (((1,), (1,)), ((), ()))
    lanes_n = lax.broadcasted_iota(I32, (ROWS, 8), 1)
    steps_n = lax.shift_right_logical(lax.broadcasted_iota(I32, (ROWS, 8), 0), 3)
    lanes_p = lax.broadcasted_iota(I32, (ROWS, 2 * PAGE), 1)

    def suffix_some(agents):
        scored = []
        for a in agents:
            at = idx_s[AGENTS, a]
            msg = jnp.where(at >= AGENTS, local[at & 31], asked[at & 31])
            new = msg[ROWS:].astype(F32)[:8]
            page0, page1 = table_ref[0, a], table_ref[1, a]
            keys = jnp.concatenate([pool[page0, :, :HEAD], pool[page1, :, :HEAD]], axis=0)
            q = msg[:ROWS]
            c = lax.dot_general(q, keys, dims, preferred_element_type=F32)
            cn = lax.dot_general(q, new.astype(BF16), dims, preferred_element_type=F32)
            scored.append((a, page0, page1, new, c, cn))
        weighed = []
        for a, page0, page1, new, c, cn in scored:
            c = jnp.where(lanes_p < pages_ref[a] * PAGE, c, LOW)
            cn = jnp.where(lanes_n <= steps_n, cn, LOW)
            peak = jnp.maximum(jnp.max(c, axis=1, keepdims=True), jnp.max(cn, axis=1, keepdims=True))
            w = jnp.exp2((c - peak) * TO_LOG2)
            wn = jnp.exp2((cn - peak) * TO_LOG2)
            total = jnp.sum(w, axis=1, keepdims=True) + jnp.sum(wn, axis=1, keepdims=True)
            weighed.append((a, page0, page1, new, peak, w.astype(BF16), wn.astype(BF16), total))
        outs = []
        for a, page0, page1, new, peak, w, wn, total in weighed:
            values = jnp.concatenate([pool[page0, :, HEAD:], pool[page1, :, HEAD:]], axis=0)
            newest = jnp.concatenate([new[4:], new[:4]], axis=0).astype(BF16)
            o = jnp.dot(w, values, preferred_element_type=F32)
            o = o + jnp.dot(wn, newest, preferred_element_type=F32)
            outs.append((a, o / total, jnp.broadcast_to(peak * TO_LOG2 + jnp.log2(total), (ROWS, HEAD))))
        for a, o, lse in outs:
            res[a] = o
            res_lse[a] = lse

    def suffix_range(first, last):
        def some(i, c):
            suffix_some([i * 8 + j for j in range(8)])
            return c
        lax.fori_loop(first // 8, last // 8, some, 0)

    def send_answers():
        lanes = lax.broadcasted_iota(I32, (ROWS, HEAD), 1)

        def one(o):
            a = idx_s[o, 0]
            ans_out[o, :, :HEAD] = res[a].astype(BF16)
            lse = res_lse[a]
            hi = lse.astype(BF16).astype(F32)
            mid = (lse - hi).astype(BF16).astype(F32)
            low = lse - hi - mid
            ans_out[o, :, HEAD:] = jnp.where(lanes < 32, hi, jnp.where(lanes < 64, mid, low)).astype(BF16)
            answer(o, o).start()
        peers(one)

    def forward_z(p):
        z_recv(p).wait_recv()
        for c in xy_send(p):
            c.start()

    def forward_xy(p):
        xy_all(p).wait_recv()
        sib_copy(p, core).start()

    own.wait()
    peak = None
    q_first = block_queries(0)
    for kc in range(TOKENS // CHUNK):
        peak = score_chunk(q_first, pre, 0, kc, peak)
    keep_peak(0, peak)

    def shard(k, c):
        p = shard_of(k)
        p_next = shard_of(jnp.minimum(k + 1, N_PRE - 1))

        @pl.when((k == 1) | ((k >= 3) & (k + 2 < N_PRE)))
        def _():
            forward_z(shard_of(jnp.where(k == 1, 4, k + 2)))

        step(0, p, 1, p)

        @pl.when(k == 0)
        def _():
            forward_z(shard_of(1))
            forward_z(shard_of(2))
            z_sends(5, N_PRE)

        @pl.when((k == 1) | ((k >= 3) & (k + 1 < N_PRE)))
        def _():
            forward_xy(shard_of(jnp.where(k == 1, 3, k + 1)))

        step(1, p, 2, p)
        step(2, p, 3, p)

        @pl.when(k == 0)
        def _():
            pool_copy.wait()
            place_agents()
            forward_xy(shard_of(1))
            suffix_range(0, 16)
            forward_z(shard_of(3))
            suffix_range(16, 32)
            forward_xy(shard_of(2))
            send_answers()

        @pl.when(k + 1 < N_PRE)
        def _():
            sib_copy(p_next, 1 - core).wait_recv()

        step(3, p, 0, p_next)
        return c

    lax.fori_loop(0, N_PRE, shard, 0)

    all_of(ans_in, rps, rpr).wait_recv()

    def finish(i, c):
        for u in range(4):
            j = i * 4 + u
            old = arrival_ref[j]
            src = lax.shift_right_logical(old, 5)
            slot = lax.rem(old, AGENTS)
            got = ans_in[src].astype(F32)
            stays = src == rep
            part = jnp.where(stays, res[slot], got[:, :HEAD])
            lse_got = got[:, HEAD:HEAD + 1] + got[:, HEAD + 32:HEAD + 33] + got[:, HEAD + 64:HEAD + 65]
            lse = jnp.where(stays, res_lse[slot], lse_got)
            rows = pl.ds(pl.multiple_of(j * ROWS, ROWS), ROWS)
            m = m_run[rows, :]
            top = jnp.maximum(m, lse)
            f, g = jnp.exp2(m - top), jnp.exp2(lse - top)
            o = (acc[rows, :] * f + part * g) / (l_run[rows, :] * f + g)
            for t in range(4):
                out_ref[t, j] = o[t * 8:(t + 1) * 8].astype(BF16)
        return c

    lax.fori_loop(0, AGENTS // 4, finish, 0)

    all_of(req_out, rqs, rqr).wait_send()
    all_of(ans_out, rps, rpr).wait_send()

    def left(p):
        z_send(p).wait_send()
        xy_all(p).wait_send()
        sib_copy(p, core).wait_send()
    planes(left)


def per_device(queries, newest_key_value, prefix_kv, suffix_pool, page_table, suffix_pages, arrival):
    vmem = pl.BlockSpec(memory_space=pltpu.VMEM)
    smem = pl.BlockSpec(memory_space=pltpu.SMEM)
    hbm = pl.BlockSpec(memory_space=pl.ANY)
    dma = pltpu.SemaphoreType.DMA
    rows = AGENTS * ROWS
    pool = suffix_pool.reshape(suffix_pool.shape[0], suffix_pool.shape[2], suffix_pool.shape[3])
    return pl.pallas_call(
        kernel,
        out_shape=jax.ShapeDtypeStruct(queries.shape, BF16),
        in_specs=[vmem, vmem, smem, smem, smem, hbm, hbm],
        out_specs=vmem,
        scratch_shapes=[
            pltpu.VMEM((N_PRE, TOKENS, 2 * HEAD), BF16),
            pltpu.VMEM((POOL, PAGE, 2 * HEAD), BF16),
            pltpu.VMEM((AGENTS, MSG, HEAD), BF16),
            pltpu.VMEM((AGENTS, 16, HEAD), F32),
            pltpu.VMEM((N_REP, MSG, HEAD), BF16),
            pltpu.VMEM((N_REP, MSG, HEAD), BF16),
            pltpu.VMEM((8, HEAD), I32),
            pltpu.SMEM((8, HEAD), I32),
            pltpu.VMEM((AGENTS + 8, HEAD), I32),
            pltpu.SMEM((AGENTS + 8, HEAD), I32),
            pltpu.VMEM((AGENTS, ROWS, HEAD), F32),
            pltpu.VMEM((AGENTS, ROWS, HEAD), F32),
            pltpu.VMEM((N_REP, ROWS, 2 * HEAD), BF16),
            pltpu.VMEM((N_REP, ROWS, 2 * HEAD), BF16),
            pltpu.VMEM((BLOCK, TOKENS), F32),
            pltpu.VMEM((BLOCK, TOKENS), F32),
            pltpu.VMEM((BLOCK, 128), F32),
            pltpu.VMEM((BLOCK, 128), F32),
            pltpu.VMEM((rows, HEAD), F32),
            pltpu.VMEM((rows, HEAD), F32),
            pltpu.VMEM((rows, HEAD), F32),
            dma((N_PRE,)), dma((N_PRE,)),
            dma((N_PRE,)), dma((N_PRE,)),
            dma((N_PRE,)), dma((N_PRE,)),
            dma((1,)), dma((1,)),
            dma((1,)), dma((1,)),
            dma((3,)),
        ],
        compiler_params=pltpu.CompilerParams(
            collective_id=0, has_side_effects=True, vmem_limit_bytes=60 << 20),
    )(queries, newest_key_value[:, :, 0, :], arrival, page_table.T, suffix_pages, prefix_kv, pool)


def solution(mesh):
    return jax.shard_map(
        per_device,
        mesh=mesh,
        in_specs=(
            P(None, "rep", "pre", None),
            P(None, "rep", "pre", None),
            P(None, "pre", None),
            P("rep", "pre", None, None),
            P("rep", None),
            P("rep"),
            P("rep"),
        ),
        out_specs=P(None, "rep", "pre", None),
        check_vma=False,
    )
```

```python
import functools

import jax
import jax.numpy as jnp
from jax import lax
from jax.experimental import pallas as pl
from jax.experimental.pallas import tpu as pltpu
from jax.sharding import PartitionSpec as P

MESH = pl.DeviceIdType.MESH
BF16 = jnp.bfloat16
F32 = jnp.float32
I32 = jnp.int32

N_REP, N_PRE = 32, 8
X_SIZE, Y_SIZE = 4, 4
TOKENS = 2048
HALF = TOKENS // 2
QUARTER = HALF // 4
AGENTS = 32
ROWS = 32
HEAD = 128
PAGE = 128
POOL = 56
MSG = 48
BLOCK = 256
BLOCKS = AGENTS * ROWS // BLOCK
CHUNK = 256
TO_LOG2 = HEAD ** (-0.5) * 1.4426950408889634
LOW = -1e30


def kernel(
    q_ref, new_ref, arrival_ref, table_ref, pages_ref, prefix_ref, pool_hbm,
    out_ref,
    kv, pool, local, tail, asked, req_out, ask_v, ask_s, idx_v, idx_s, res, res_lse, ans_out, ans_in,
    s0, s1, m0, m1, acc, m_run, l_run,
    zs, zr, xs, xr, ss, sr, rqs, rqr, rps, rpr, loc,
):
    rep = lax.axis_index("rep")
    pre = lax.axis_index("pre")
    core = lax.rem(rep, 2)
    x = lax.rem(rep // 2, X_SIZE)
    y = rep // (2 * X_SIZE)
    sibling = rep + 1 - 2 * core

    def at_xy(xx, yy):
        return (lax.rem(yy + Y_SIZE, Y_SIZE) * X_SIZE + lax.rem(xx + X_SIZE, X_SIZE)) * 2 + core

    x_up, x_down = at_xy(x + 1, y), at_xy(x - 1, y)
    y_up, y_down = at_xy(x, y + 1), at_xy(x, y - 1)
    swap = core == 1
    a_up, a_down = jnp.where(swap, y_up, x_up), jnp.where(swap, y_down, x_down)
    b_up, b_down = jnp.where(swap, x_up, y_up), jnp.where(swap, x_down, y_down)
    mine = lax.rem(jnp.where(swap, y + 2 * x, x + 2 * y), 4)

    def spot(which, size=QUARTER, extra=0):
        start = core * HALF + lax.rem(which + 4, 4) * QUARTER + extra
        return pl.ds(pl.multiple_of(start, 128), size)

    def shard_of(k):
        k = jnp.int32(k)
        far = (k + 1) // 2
        return lax.rem(pre + jnp.where(lax.rem(k, 2) == 1, far, -far) + N_PRE, N_PRE)

    def z_send(plane):
        where = spot(mine)
        return pltpu.make_async_remote_copy(
            src_ref=prefix_ref.at[plane, where, :], dst_ref=kv.at[pre, where, :],
            send_sem=zs.at[plane], recv_sem=zr.at[pre], device_id=(rep, plane), device_id_type=MESH)

    def z_recv(p):
        where = spot(mine)
        return pltpu.make_async_remote_copy(
            src_ref=kv.at[p, where, :], dst_ref=kv.at[p, where, :],
            send_sem=zs.at[p], recv_sem=zr.at[p], device_id=(rep, p), device_id_type=MESH)

    def xy_copies(p, which, who):
        out = []
        for i, (size, extra) in enumerate(
            ((QUARTER, 0), (QUARTER, 0), (QUARTER // 2, 0), (QUARTER // 2, QUARTER // 2))
        ):
            ref = kv.at[p, spot(which[i], size, extra), :]
            out.append(pltpu.make_async_remote_copy(
                src_ref=ref, dst_ref=ref, send_sem=xs.at[p], recv_sem=xr.at[p],
                device_id=(who[i], pre), device_id_type=MESH))
        return out

    def xy_send(p):
        return xy_copies(p, (mine, mine, mine, mine), (a_up, a_down, b_up, b_down))

    def xy_all(p):
        ref = kv.at[p, pl.ds(0, 3 * QUARTER), :]
        return pltpu.make_async_remote_copy(
            src_ref=ref, dst_ref=ref, send_sem=xs.at[p], recv_sem=xr.at[p],
            device_id=(a_up, pre), device_id_type=MESH)

    def sib_copy(p, half):
        ref = kv.at[p, pl.ds(pl.multiple_of(half * HALF, HALF), HALF), :]
        return pltpu.make_async_remote_copy(
            src_ref=ref, dst_ref=ref, send_sem=ss.at[p], recv_sem=sr.at[p],
            device_id=(sibling, pre), device_id_type=MESH)

    def request(slot, other):
        return pltpu.make_async_remote_copy(
            src_ref=req_out.at[slot], dst_ref=asked.at[rep],
            send_sem=rqs.at[0], recv_sem=rqr.at[0], device_id=(other, pre), device_id_type=MESH)

    def answer(slot, other):
        return pltpu.make_async_remote_copy(
            src_ref=ans_out.at[slot], dst_ref=ans_in.at[rep],
            send_sem=rps.at[0], recv_sem=rpr.at[0], device_id=(other, pre), device_id_type=MESH)

    def all_of(buf, send, recv):
        ref = buf.at[pl.ds(0, N_REP - 1)]
        return pltpu.make_async_remote_copy(
            src_ref=ref, dst_ref=ref, send_sem=send.at[0], recv_sem=recv.at[0],
            device_id=(sibling, pre), device_id_type=MESH)

    def peers(fn):
        def one(i, c):
            fn(lax.rem(rep + i, N_REP))
            return c
        lax.fori_loop(1, N_REP, one, 0)

    def planes(fn):
        def one(k, c):
            fn(shard_of(k))
            return c
        lax.fori_loop(1, N_PRE, one, 0)

    own = pltpu.make_async_copy(prefix_ref.at[pre], kv.at[pre], loc.at[0])
    own.start()
    pool_copy = pltpu.make_async_copy(pool_hbm, pool, loc.at[1])
    pool_copy.start()
    barrier = pltpu.get_barrier_semaphore()
    peers(lambda o: pl.semaphore_signal(barrier, inc=1, device_id=(o, pre), device_id_type=MESH))
    planes(lambda p: pl.semaphore_signal(barrier, inc=1, device_id=(rep, p), device_id_type=MESH))

    lane = lax.broadcasted_iota(I32, (AGENTS, HEAD), 1)
    sub = lax.broadcasted_iota(I32, (AGENTS, HEAD), 0)
    old = jnp.zeros((AGENTS, HEAD), I32)
    for j in range(AGENTS):
        old = jnp.where(sub == j, arrival_ref[j], old)
    from_rep = lax.shift_right_logical(old, 5)
    asker = jnp.max(jnp.where(from_rep == lane, sub, 0), axis=0, keepdims=True)
    ask_v[...] = jnp.broadcast_to(asker, (8, HEAD))
    ask_put = pltpu.make_async_copy(ask_v, ask_s, loc.at[2])
    ask_put.start()

    pl.semaphore_wait(barrier, N_REP - 1 + N_PRE - 1)

    def z_sends(first, last):
        def one(k, c):
            z_send(shard_of(k)).start()
            return c
        lax.fori_loop(first, last, one, 0)
    z_sends(1, 5)

    for t in range(4):
        tail[:, t, :] = new_ref[t, :, :HEAD].astype(F32)
        tail[:, 4 + t, :] = new_ref[t, :, HEAD:].astype(F32)
    tail[:, 8, :] = (old & 31).astype(F32)
    tail[:, 9, :] = from_rep.astype(F32)
    for t in range(10, 16):
        tail[:, t, :] = jnp.zeros((AGENTS, HEAD), F32)

    def build(i, c):
        for u in range(8):
            j = i * 8 + u
            rows = jnp.concatenate([q_ref[t, j].astype(F32) for t in range(4)] + [tail[j]], axis=0)
            local[j] = rows.astype(BF16)
        return c
    lax.fori_loop(0, AGENTS // 8, build, 0)

    ask_put.wait()

    def ask(o):
        req_out[o] = local[ask_s[0, o]]
        request(o, o).start()
    peers(ask)
    asked[rep] = jnp.zeros((MSG, HEAD), BF16)
    ans_in[rep] = jnp.zeros((ROWS, 2 * HEAD), BF16)

    m_run[...] = jnp.full_like(m_run, LOW)
    l_run[...] = jnp.zeros_like(l_run)
    acc[...] = jnp.zeros_like(acc)
    score_bufs, peak_bufs = (s0, s1), (m0, m1)
    per = BLOCK // ROWS

    def block_queries(b):
        return local[b * per:(b + 1) * per, :ROWS, :].reshape(BLOCK, HEAD)

    def score_chunk(q, p, u, kc, peak):
        k = kv[p, kc * CHUNK:(kc + 1) * CHUNK, :HEAD]
        s = lax.dot_general(q, k, (((1,), (1,)), ((), ())), preferred_element_type=F32)
        score_bufs[u][:, kc * CHUNK:(kc + 1) * CHUNK] = s
        for j in range(CHUNK // 128):
            part = s[:, j * 128:(j + 1) * 128]
            peak = part if peak is None else jnp.maximum(peak, part)
        return peak

    def keep_peak(u, peak):
        peak_bufs[u][...] = jnp.broadcast_to(jnp.max(peak, axis=1, keepdims=True), (BLOCK, 128))

    ones = jnp.ones((CHUNK, HEAD), BF16)

    def step(b, p, b_next, p_next, beside=None):
        u, v = b % 2, b_next % 2
        q = block_queries(b_next)
        peak = peak_bufs[u][:, :1]
        nxt = None
        out = None

        def values(kc, w):
            both = jnp.concatenate([kv[p, kc * CHUNK:(kc + 1) * CHUNK, HEAD:], ones], axis=1)
            d = jnp.dot(w, both, preferred_element_type=F32)
            return d if out is None else out + d

        last = None
        for kc in range(TOKENS // CHUNK):
            w = jnp.exp2((score_bufs[u][:, kc * CHUNK:(kc + 1) * CHUNK] - peak) * TO_LOG2).astype(BF16)
            nxt = score_chunk(q, p_next, v, kc, nxt)
            if last is not None:
                out = values(kc - 1, last)
            last = w
            if beside is not None:
                beside(kc)
        out = values(TOKENS // CHUNK - 1, last)
        keep_peak(v, nxt)
        rows = slice(b * BLOCK, (b + 1) * BLOCK)
        top = peak_bufs[u][...] * TO_LOG2
        old = m_run[rows, :]
        new = jnp.maximum(old, top)
        f_old, f_new = jnp.exp2(old - new), jnp.exp2(top - new)
        m_run[rows, :] = new
        l_run[rows, :] = l_run[rows, :] * f_old + out[:, HEAD:] * f_new
        acc[rows, :] = acc[rows, :] * f_old + out[:, :HEAD] * f_new

    def place_agents():
        all_of(asked, rqs, rqr).wait_recv()
        told = asked[:, ROWS:, :].astype(F32)
        slots = told[:, 8, :].astype(I32)
        reps = told[:, 9, :].astype(I32)
        for_me = (reps == rep) & (sub != rep)
        moved = jnp.where(for_me & (slots == lane), sub, 0)
        stays = jnp.where((from_rep == rep) & ((old & 31) == lane), sub + AGENTS, 0)
        at = jnp.max(jnp.maximum(moved, stays), axis=0, keepdims=True)
        idx_v[:AGENTS, :] = jnp.where(for_me, slots & 31, 0)
        idx_v[AGENTS:, :] = jnp.broadcast_to(at, (8, HEAD))
        put = pltpu.make_async_copy(idx_v, idx_s, loc.at[2])
        put.start()
        put.wait()

    dims = (((1,), (1,)), ((), ()))
    lanes_n = lax.broadcasted_iota(I32, (ROWS, 8), 1)
    steps_n = lax.shift_right_logical(lax.broadcasted_iota(I32, (ROWS, 8), 0), 3)
    lanes_p = lax.broadcasted_iota(I32, (ROWS, 2 * PAGE), 1)

    def suffix_some(agents):
        scored = []
        for a in agents:
            at = idx_s[AGENTS, a]
            msg = jnp.where(at >= AGENTS, local[at & 31], asked[at & 31])
            new = msg[ROWS:].astype(F32)[:8]
            page0, page1 = table_ref[0, a], table_ref[1, a]
            keys = jnp.concatenate([pool[page0, :, :HEAD], pool[page1, :, :HEAD]], axis=0)
            q = msg[:ROWS]
            c = lax.dot_general(q, keys, dims, preferred_element_type=F32)
            cn = lax.dot_general(q, new.astype(BF16), dims, preferred_element_type=F32)
            scored.append((a, page0, page1, new, c, cn))
        weighed = []
        for a, page0, page1, new, c, cn in scored:
            c = jnp.where(lanes_p < pages_ref[a] * PAGE, c, LOW)
            cn = jnp.where(lanes_n <= steps_n, cn, LOW)
            peak = jnp.maximum(jnp.max(c, axis=1, keepdims=True), jnp.max(cn, axis=1, keepdims=True))
            w = jnp.exp2((c - peak) * TO_LOG2)
            wn = jnp.exp2((cn - peak) * TO_LOG2)
            total = jnp.sum(w, axis=1, keepdims=True) + jnp.sum(wn, axis=1, keepdims=True)
            weighed.append((a, page0, page1, new, peak, w.astype(BF16), wn.astype(BF16), total))
        outs = []
        for a, page0, page1, new, peak, w, wn, total in weighed:
            values = jnp.concatenate([pool[page0, :, HEAD:], pool[page1, :, HEAD:]], axis=0)
            newest = jnp.concatenate([new[4:], new[:4]], axis=0).astype(BF16)
            o = jnp.dot(w, values, preferred_element_type=F32)
            o = o + jnp.dot(wn, newest, preferred_element_type=F32)
            outs.append((a, o / total, jnp.broadcast_to(peak * TO_LOG2 + jnp.log2(total), (ROWS, HEAD))))
        for a, o, lse in outs:
            res[a] = o
            res_lse[a] = lse

    def suffix_range(first, last):
        def some(i, c):
            suffix_some([i * 8 + j for j in range(8)])
            return c
        lax.fori_loop(first // 8, last // 8, some, 0)

    answer_lanes = lax.broadcasted_iota(I32, (ROWS, HEAD), 1)

    def send_answer(i):
        o = lax.rem(rep + i, N_REP)
        a = idx_s[o, 0]
        ans_out[o, :, :HEAD] = res[a].astype(BF16)
        lse = res_lse[a]
        hi = lse.astype(BF16).astype(F32)
        mid = (lse - hi).astype(BF16).astype(F32)
        low = lse - hi - mid
        ans_out[o, :, HEAD:] = jnp.where(
            answer_lanes < 32, hi, jnp.where(answer_lanes < 64, mid, low)).astype(BF16)
        answer(o, o).start()

    def forward_z(p):
        z_recv(p).wait_recv()
        for c in xy_send(p):
            c.start()

    def forward_xy(p):
        xy_all(p).wait_recv()
        sib_copy(p, core).start()

    own.wait()
    peak = None
    q_first = block_queries(0)
    for kc in range(TOKENS // CHUNK):
        peak = score_chunk(q_first, pre, 0, kc, peak)
    keep_peak(0, peak)

    def next_arrived(p):
        sib_copy(p, 1 - core).wait_recv()

    first, second = shard_of(1), shard_of(2)
    step(0, pre, 1, pre)
    forward_z(first)
    forward_z(second)
    z_sends(5, N_PRE)
    step(1, pre, 2, pre)
    step(2, pre, 3, pre)
    pool_copy.wait()
    place_agents()
    forward_z(shard_of(3))
    forward_z(shard_of(4))
    forward_xy(first)
    suffix_range(0, 16)
    forward_xy(second)
    suffix_range(16, 32)
    def all_answers(i, c):
        send_answer(i)
        return c
    lax.fori_loop(1, N_REP, all_answers, 0)
    next_arrived(first)
    step(3, pre, 0, first)

    passed = {
        (1, 1): (forward_xy, 3), (1, 3): (forward_xy, 4),
        (2, 1): (forward_z, 5), (2, 2): (forward_z, 6),
        (3, 2): (forward_xy, 5), (4, 0): (forward_z, 7),
        (4, 1): (forward_xy, 6), (5, 2): (forward_xy, 7),
    }

    def shard(k, c):
        p = shard_of(k)
        p_next = shard_of(jnp.minimum(k + 1, N_PRE - 1))
        for b in range(BLOCKS):
            for (at, ahead_of), (pass_on, which) in passed.items():
                if ahead_of == b:
                    pl.when(k == at)(functools.partial(pass_on, shard_of(which)))
            if b == BLOCKS - 1:
                pl.when(k + 1 < N_PRE)(functools.partial(next_arrived, p_next))
                step(b, p, 0, p_next)
            else:
                step(b, p, b + 1, p)
        return c

    lax.fori_loop(1, N_PRE, shard, 0)

    all_of(ans_in, rps, rpr).wait_recv()

    def finish(i, c):
        for u in range(8):
            j = i * 8 + u
            old = arrival_ref[j]
            src = lax.shift_right_logical(old, 5)
            slot = lax.rem(old, AGENTS)
            got = ans_in[src].astype(F32)
            stays = src == rep
            part = jnp.where(stays, res[slot], got[:, :HEAD])
            lse_got = got[:, HEAD:HEAD + 1] + got[:, HEAD + 32:HEAD + 33] + got[:, HEAD + 64:HEAD + 65]
            lse = jnp.where(stays, res_lse[slot], lse_got)
            rows = pl.ds(pl.multiple_of(j * ROWS, ROWS), ROWS)
            m = m_run[rows, :]
            top = jnp.maximum(m, lse)
            f, g = jnp.exp2(m - top), jnp.exp2(lse - top)
            o = (acc[rows, :] * f + part * g) / (l_run[rows, :] * f + g)
            for t in range(4):
                out_ref[t, j] = o[t * 8:(t + 1) * 8].astype(BF16)
        return c

    lax.fori_loop(0, AGENTS // 8, finish, 0)

    all_of(req_out, rqs, rqr).wait_send()
    all_of(ans_out, rps, rpr).wait_send()

    def left(p):
        z_send(p).wait_send()
        xy_all(p).wait_send()
        sib_copy(p, core).wait_send()
    planes(left)


def per_device(queries, newest_key_value, prefix_kv, suffix_pool, page_table, suffix_pages, arrival):
    vmem = pl.BlockSpec(memory_space=pltpu.VMEM)
    smem = pl.BlockSpec(memory_space=pltpu.SMEM)
    hbm = pl.BlockSpec(memory_space=pl.ANY)
    dma = pltpu.SemaphoreType.DMA
    rows = AGENTS * ROWS
    pool = suffix_pool.reshape(suffix_pool.shape[0], suffix_pool.shape[2], suffix_pool.shape[3])
    return pl.pallas_call(
        kernel,
        out_shape=jax.ShapeDtypeStruct(queries.shape, BF16),
        in_specs=[vmem, vmem, smem, smem, smem, hbm, hbm],
        out_specs=vmem,
        scratch_shapes=[
            pltpu.VMEM((N_PRE, TOKENS, 2 * HEAD), BF16),
            pltpu.VMEM((POOL, PAGE, 2 * HEAD), BF16),
            pltpu.VMEM((AGENTS, MSG, HEAD), BF16),
            pltpu.VMEM((AGENTS, 16, HEAD), F32),
            pltpu.VMEM((N_REP, MSG, HEAD), BF16),
            pltpu.VMEM((N_REP, MSG, HEAD), BF16),
            pltpu.VMEM((8, HEAD), I32),
            pltpu.SMEM((8, HEAD), I32),
            pltpu.VMEM((AGENTS + 8, HEAD), I32),
            pltpu.SMEM((AGENTS + 8, HEAD), I32),
            pltpu.VMEM((AGENTS, ROWS, HEAD), F32),
            pltpu.VMEM((AGENTS, ROWS, HEAD), F32),
            pltpu.VMEM((N_REP, ROWS, 2 * HEAD), BF16),
            pltpu.VMEM((N_REP, ROWS, 2 * HEAD), BF16),
            pltpu.VMEM((BLOCK, TOKENS), F32),
            pltpu.VMEM((BLOCK, TOKENS), F32),
            pltpu.VMEM((BLOCK, 128), F32),
            pltpu.VMEM((BLOCK, 128), F32),
            pltpu.VMEM((rows, HEAD), F32),
            pltpu.VMEM((rows, HEAD), F32),
            pltpu.VMEM((rows, HEAD), F32),
            dma((N_PRE,)), dma((N_PRE,)),
            dma((N_PRE,)), dma((N_PRE,)),
            dma((N_PRE,)), dma((N_PRE,)),
            dma((1,)), dma((1,)),
            dma((1,)), dma((1,)),
            dma((3,)),
        ],
        compiler_params=pltpu.CompilerParams(
            collective_id=0, has_side_effects=True, vmem_limit_bytes=60 << 20),
    )(queries, newest_key_value[:, :, 0, :], arrival, page_table.T, suffix_pages, prefix_kv, pool)


def solution(mesh):
    return jax.shard_map(
        per_device,
        mesh=mesh,
        in_specs=(
            P(None, "rep", "pre", None),
            P(None, "rep", "pre", None),
            P(None, "pre", None),
            P("rep", "pre", None, None),
            P("rep", None),
            P("rep"),
            P("rep"),
        ),
        out_specs=P(None, "rep", "pre", None),
        check_vma=False,
    )
```

```python
import functools

import jax
import jax.numpy as jnp
from jax import lax
from jax.experimental import pallas as pl
from jax.experimental.pallas import tpu as pltpu
from jax.sharding import PartitionSpec as P

MESH = pl.DeviceIdType.MESH
BF16 = jnp.bfloat16
F32 = jnp.float32
I32 = jnp.int32

N_REP, N_PRE = 32, 8
X_SIZE, Y_SIZE = 4, 4
TOKENS = 2048
HALF = TOKENS // 2
QUARTER = HALF // 4
AGENTS = 32
ROWS = 32
HEAD = 128
PAGE = 128
POOL = 56
MSG = 48
BLOCK = 512
BLOCKS = AGENTS * ROWS // BLOCK
CHUNK = 256
TO_LOG2 = HEAD ** (-0.5) * 1.4426950408889634
LOW = -1e30


def kernel(
    q_ref, new_ref, arrival_ref, table_ref, pages_ref, prefix_ref, pool_hbm,
    out_ref,
    kv, pool, local, tail, asked, req_out, ask_v, ask_s, idx_v, idx_s, res, res_lse, ans_out, ans_in,
    s0, s1, m0, m1, acc, m_run, l_run,
    zs, zr, xs, xr, ss, sr, rqs, rqr, rps, rpr, loc,
):
    rep = lax.axis_index("rep")
    pre = lax.axis_index("pre")
    core = lax.rem(rep, 2)
    x = lax.rem(rep // 2, X_SIZE)
    y = rep // (2 * X_SIZE)
    sibling = rep + 1 - 2 * core

    def at_xy(xx, yy):
        return (lax.rem(yy + Y_SIZE, Y_SIZE) * X_SIZE + lax.rem(xx + X_SIZE, X_SIZE)) * 2 + core

    x_up, x_down = at_xy(x + 1, y), at_xy(x - 1, y)
    y_up, y_down = at_xy(x, y + 1), at_xy(x, y - 1)
    swap = core == 1
    a_up, a_down = jnp.where(swap, y_up, x_up), jnp.where(swap, y_down, x_down)
    b_up, b_down = jnp.where(swap, x_up, y_up), jnp.where(swap, x_down, y_down)
    mine = lax.rem(jnp.where(swap, y + 2 * x, x + 2 * y), 4)

    def spot(which, size=QUARTER, extra=0):
        start = core * HALF + lax.rem(which + 4, 4) * QUARTER + extra
        return pl.ds(pl.multiple_of(start, 128), size)

    def shard_of(k):
        k = jnp.int32(k)
        far = (k + 1) // 2
        return lax.rem(pre + jnp.where(lax.rem(k, 2) == 1, far, -far) + N_PRE, N_PRE)

    def z_send(plane):
        where = spot(mine)
        return pltpu.make_async_remote_copy(
            src_ref=prefix_ref.at[plane, where, :], dst_ref=kv.at[pre, where, :],
            send_sem=zs.at[plane], recv_sem=zr.at[pre], device_id=(rep, plane), device_id_type=MESH)

    def z_recv(p):
        where = spot(mine)
        return pltpu.make_async_remote_copy(
            src_ref=kv.at[p, where, :], dst_ref=kv.at[p, where, :],
            send_sem=zs.at[p], recv_sem=zr.at[p], device_id=(rep, p), device_id_type=MESH)

    def xy_copies(p, which, who):
        out = []
        for i, (size, extra) in enumerate(
            ((QUARTER, 0), (QUARTER, 0), (QUARTER // 2, 0), (QUARTER // 2, QUARTER // 2))
        ):
            ref = kv.at[p, spot(which[i], size, extra), :]
            out.append(pltpu.make_async_remote_copy(
                src_ref=ref, dst_ref=ref, send_sem=xs.at[p], recv_sem=xr.at[p],
                device_id=(who[i], pre), device_id_type=MESH))
        return out

    def xy_send(p):
        return xy_copies(p, (mine, mine, mine, mine), (a_up, a_down, b_up, b_down))

    def xy_all(p):
        ref = kv.at[p, pl.ds(0, 3 * QUARTER), :]
        return pltpu.make_async_remote_copy(
            src_ref=ref, dst_ref=ref, send_sem=xs.at[p], recv_sem=xr.at[p],
            device_id=(a_up, pre), device_id_type=MESH)

    def sib_copy(p, half):
        ref = kv.at[p, pl.ds(pl.multiple_of(half * HALF, HALF), HALF), :]
        return pltpu.make_async_remote_copy(
            src_ref=ref, dst_ref=ref, send_sem=ss.at[p], recv_sem=sr.at[p],
            device_id=(sibling, pre), device_id_type=MESH)

    def request(slot, other):
        return pltpu.make_async_remote_copy(
            src_ref=req_out.at[slot], dst_ref=asked.at[rep],
            send_sem=rqs.at[0], recv_sem=rqr.at[0], device_id=(other, pre), device_id_type=MESH)

    def answer(slot, other):
        return pltpu.make_async_remote_copy(
            src_ref=ans_out.at[slot], dst_ref=ans_in.at[rep],
            send_sem=rps.at[0], recv_sem=rpr.at[0], device_id=(other, pre), device_id_type=MESH)

    def all_of(buf, send, recv):
        ref = buf.at[pl.ds(0, N_REP - 1)]
        return pltpu.make_async_remote_copy(
            src_ref=ref, dst_ref=ref, send_sem=send.at[0], recv_sem=recv.at[0],
            device_id=(sibling, pre), device_id_type=MESH)

    def peers(fn):
        def one(i, c):
            fn(lax.rem(rep + i, N_REP))
            return c
        lax.fori_loop(1, N_REP, one, 0)

    def planes(fn):
        def one(k, c):
            fn(shard_of(k))
            return c
        lax.fori_loop(1, N_PRE, one, 0)

    own = pltpu.make_async_copy(prefix_ref.at[pre], kv.at[pre], loc.at[0])
    own.start()
    pool_copy = pltpu.make_async_copy(pool_hbm, pool, loc.at[1])
    pool_copy.start()
    barrier = pltpu.get_barrier_semaphore()
    peers(lambda o: pl.semaphore_signal(barrier, inc=1, device_id=(o, pre), device_id_type=MESH))
    planes(lambda p: pl.semaphore_signal(barrier, inc=1, device_id=(rep, p), device_id_type=MESH))

    lane = lax.broadcasted_iota(I32, (AGENTS, HEAD), 1)
    sub = lax.broadcasted_iota(I32, (AGENTS, HEAD), 0)
    old = jnp.zeros((AGENTS, HEAD), I32)
    for j in range(AGENTS):
        old = jnp.where(sub == j, arrival_ref[j], old)
    from_rep = lax.shift_right_logical(old, 5)
    asker = jnp.max(jnp.where(from_rep == lane, sub, 0), axis=0, keepdims=True)
    ask_v[...] = jnp.broadcast_to(asker, (8, HEAD))
    ask_put = pltpu.make_async_copy(ask_v, ask_s, loc.at[2])
    ask_put.start()

    pl.semaphore_wait(barrier, N_REP - 1 + N_PRE - 1)

    def z_sends(first, last):
        def one(k, c):
            z_send(shard_of(k)).start()
            return c
        lax.fori_loop(first, last, one, 0)
    z_sends(1, 5)

    for t in range(4):
        tail[:, t, :] = new_ref[t, :, :HEAD].astype(F32)
        tail[:, 4 + t, :] = new_ref[t, :, HEAD:].astype(F32)
    tail[:, 8, :] = (old & 31).astype(F32)
    tail[:, 9, :] = from_rep.astype(F32)
    for t in range(10, 16):
        tail[:, t, :] = jnp.zeros((AGENTS, HEAD), F32)

    def build(i, c):
        for u in range(8):
            j = i * 8 + u
            rows = jnp.concatenate([q_ref[t, j].astype(F32) for t in range(4)] + [tail[j]], axis=0)
            local[j] = rows.astype(BF16)
        return c
    lax.fori_loop(0, AGENTS // 8, build, 0)

    ask_put.wait()

    def ask(o):
        req_out[o] = local[ask_s[0, o]]
        request(o, o).start()
    peers(ask)
    asked[rep] = jnp.zeros((MSG, HEAD), BF16)
    ans_in[rep] = jnp.zeros((ROWS, 2 * HEAD), BF16)

    m_run[...] = jnp.full_like(m_run, LOW)
    l_run[...] = jnp.zeros_like(l_run)
    acc[...] = jnp.zeros_like(acc)
    score_bufs, peak_bufs = (s0, s1), (m0, m1)
    per = BLOCK // ROWS

    def block_queries(b):
        return local[b * per:(b + 1) * per, :ROWS, :].reshape(BLOCK, HEAD)

    def score_chunk(q, p, u, kc, peak):
        k = kv[p, kc * CHUNK:(kc + 1) * CHUNK, :HEAD]
        s = lax.dot_general(q, k, (((1,), (1,)), ((), ())), preferred_element_type=F32)
        score_bufs[u][:, kc * CHUNK:(kc + 1) * CHUNK] = s
        for j in range(CHUNK // 128):
            part = s[:, j * 128:(j + 1) * 128]
            peak = part if peak is None else jnp.maximum(peak, part)
        return peak

    def keep_peak(u, peak):
        peak_bufs[u][...] = jnp.broadcast_to(jnp.max(peak, axis=1, keepdims=True), (BLOCK, 128))

    ones = jnp.ones((CHUNK, HEAD), BF16)

    def step(b, p, b_next, p_next, beside=None):
        u, v = b % 2, b_next % 2
        q = block_queries(b_next)
        peak = peak_bufs[u][:, :1]
        nxt = None
        out = None

        def values(kc, w):
            both = jnp.concatenate([kv[p, kc * CHUNK:(kc + 1) * CHUNK, HEAD:], ones], axis=1)
            d = jnp.dot(w, both, preferred_element_type=F32)
            return d if out is None else out + d

        last = None
        for kc in range(TOKENS // CHUNK):
            w = jnp.exp2((score_bufs[u][:, kc * CHUNK:(kc + 1) * CHUNK] - peak) * TO_LOG2).astype(BF16)
            nxt = score_chunk(q, p_next, v, kc, nxt)
            if last is not None:
                out = values(kc - 1, last)
            last = w
            if beside is not None:
                beside(kc)
        out = values(TOKENS // CHUNK - 1, last)
        keep_peak(v, nxt)
        rows = slice(b * BLOCK, (b + 1) * BLOCK)
        top = peak_bufs[u][...] * TO_LOG2
        old = m_run[rows, :]
        new = jnp.maximum(old, top)
        f_old, f_new = jnp.exp2(old - new), jnp.exp2(top - new)
        m_run[rows, :] = new
        l_run[rows, :] = l_run[rows, :] * f_old + out[:, HEAD:] * f_new
        acc[rows, :] = acc[rows, :] * f_old + out[:, :HEAD] * f_new

    def place_agents():
        all_of(asked, rqs, rqr).wait_recv()
        told = asked[:, ROWS:, :].astype(F32)
        slots = told[:, 8, :].astype(I32)
        reps = told[:, 9, :].astype(I32)
        for_me = (reps == rep) & (sub != rep)
        moved = jnp.where(for_me & (slots == lane), sub, 0)
        stays = jnp.where((from_rep == rep) & ((old & 31) == lane), sub + AGENTS, 0)
        at = jnp.max(jnp.maximum(moved, stays), axis=0, keepdims=True)
        idx_v[:AGENTS, :] = jnp.where(for_me, slots & 31, 0)
        idx_v[AGENTS:, :] = jnp.broadcast_to(at, (8, HEAD))
        put = pltpu.make_async_copy(idx_v, idx_s, loc.at[2])
        put.start()
        put.wait()

    dims = (((1,), (1,)), ((), ()))
    lanes_n = lax.broadcasted_iota(I32, (ROWS, 8), 1)
    steps_n = lax.shift_right_logical(lax.broadcasted_iota(I32, (ROWS, 8), 0), 3)
    lanes_p = lax.broadcasted_iota(I32, (ROWS, 2 * PAGE), 1)

    def suffix_some(agents):
        scored = []
        for a in agents:
            at = idx_s[AGENTS, a]
            msg = jnp.where(at >= AGENTS, local[at & 31], asked[at & 31])
            new = msg[ROWS:].astype(F32)[:8]
            page0, page1 = table_ref[0, a], table_ref[1, a]
            keys = jnp.concatenate([pool[page0, :, :HEAD], pool[page1, :, :HEAD]], axis=0)
            q = msg[:ROWS]
            c = lax.dot_general(q, keys, dims, preferred_element_type=F32)
            cn = lax.dot_general(q, new.astype(BF16), dims, preferred_element_type=F32)
            scored.append((a, page0, page1, new, c, cn))
        weighed = []
        for a, page0, page1, new, c, cn in scored:
            c = jnp.where(lanes_p < pages_ref[a] * PAGE, c, LOW)
            cn = jnp.where(lanes_n <= steps_n, cn, LOW)
            peak = jnp.maximum(jnp.max(c, axis=1, keepdims=True), jnp.max(cn, axis=1, keepdims=True))
            w = jnp.exp2((c - peak) * TO_LOG2)
            wn = jnp.exp2((cn - peak) * TO_LOG2)
            total = jnp.sum(w, axis=1, keepdims=True) + jnp.sum(wn, axis=1, keepdims=True)
            weighed.append((a, page0, page1, new, peak, w.astype(BF16), wn.astype(BF16), total))
        outs = []
        for a, page0, page1, new, peak, w, wn, total in weighed:
            values = jnp.concatenate([pool[page0, :, HEAD:], pool[page1, :, HEAD:]], axis=0)
            newest = jnp.concatenate([new[4:], new[:4]], axis=0).astype(BF16)
            o = jnp.dot(w, values, preferred_element_type=F32)
            o = o + jnp.dot(wn, newest, preferred_element_type=F32)
            outs.append((a, o / total, jnp.broadcast_to(peak * TO_LOG2 + jnp.log2(total), (ROWS, HEAD))))
        for a, o, lse in outs:
            res[a] = o
            res_lse[a] = lse

    def suffix_range(first, last):
        def some(i, c):
            suffix_some([i * 8 + j for j in range(8)])
            return c
        lax.fori_loop(first // 8, last // 8, some, 0)

    answer_lanes = lax.broadcasted_iota(I32, (ROWS, HEAD), 1)

    def send_answer(i):
        o = lax.rem(rep + i, N_REP)
        a = idx_s[o, 0]
        ans_out[o, :, :HEAD] = res[a].astype(BF16)
        lse = res_lse[a]
        hi = lse.astype(BF16).astype(F32)
        mid = (lse - hi).astype(BF16).astype(F32)
        low = lse - hi - mid
        ans_out[o, :, HEAD:] = jnp.where(
            answer_lanes < 32, hi, jnp.where(answer_lanes < 64, mid, low)).astype(BF16)
        answer(o, o).start()

    def forward_z(p):
        z_recv(p).wait_recv()
        for c in xy_send(p):
            c.start()

    def forward_xy(p):
        xy_all(p).wait_recv()
        sib_copy(p, core).start()

    own.wait()
    peak = None
    q_first = block_queries(0)
    for kc in range(TOKENS // CHUNK):
        peak = score_chunk(q_first, pre, 0, kc, peak)
    keep_peak(0, peak)

    def next_arrived(p):
        sib_copy(p, 1 - core).wait_recv()

    first, second = shard_of(1), shard_of(2)
    forward_z(first)
    forward_z(second)
    z_sends(5, N_PRE)
    step(0, pre, 1, pre)
    pool_copy.wait()
    place_agents()
    forward_z(shard_of(3))
    forward_z(shard_of(4))
    forward_xy(first)
    suffix_range(0, 16)
    forward_xy(second)
    suffix_range(16, 32)
    def all_answers(i, c):
        send_answer(i)
        return c
    lax.fori_loop(1, N_REP, all_answers, 0)
    next_arrived(first)
    step(1, pre, 0, first)

    passed = {
        (1, 0): (forward_xy, 3), (1, 1): (forward_xy, 4),
        (2, 0): (forward_z, 5), (2, 1): (forward_z, 6),
        (3, 1): (forward_xy, 5), (4, 0): (forward_z, 7),
        (4, 1): (forward_xy, 6), (5, 1): (forward_xy, 7),
    }

    def shard(k, c):
        p = shard_of(k)
        p_next = shard_of(jnp.minimum(k + 1, N_PRE - 1))
        for b in range(BLOCKS):
            for (at, ahead_of), (pass_on, which) in passed.items():
                if ahead_of == b:
                    pl.when(k == at)(functools.partial(pass_on, shard_of(which)))
            if b == BLOCKS - 1:
                pl.when(k + 1 < N_PRE)(functools.partial(next_arrived, p_next))
                step(b, p, 0, p_next)
            else:
                step(b, p, b + 1, p)
        return c

    lax.fori_loop(1, N_PRE, shard, 0)

    all_of(ans_in, rps, rpr).wait_recv()

    def finish(i, c):
        for u in range(8):
            j = i * 8 + u
            old = arrival_ref[j]
            src = lax.shift_right_logical(old, 5)
            slot = lax.rem(old, AGENTS)
            got = ans_in[src].astype(F32)
            stays = src == rep
            part = jnp.where(stays, res[slot], got[:, :HEAD])
            lse_got = got[:, HEAD:HEAD + 1] + got[:, HEAD + 32:HEAD + 33] + got[:, HEAD + 64:HEAD + 65]
            lse = jnp.where(stays, res_lse[slot], lse_got)
            rows = pl.ds(pl.multiple_of(j * ROWS, ROWS), ROWS)
            m = m_run[rows, :]
            top = jnp.maximum(m, lse)
            f, g = jnp.exp2(m - top), jnp.exp2(lse - top)
            o = (acc[rows, :] * f + part * g) / (l_run[rows, :] * f + g)
            for t in range(4):
                out_ref[t, j] = o[t * 8:(t + 1) * 8].astype(BF16)
        return c

    lax.fori_loop(0, AGENTS // 8, finish, 0)

    all_of(req_out, rqs, rqr).wait_send()
    all_of(ans_out, rps, rpr).wait_send()

    def left(p):
        z_send(p).wait_send()
        xy_all(p).wait_send()
        sib_copy(p, core).wait_send()
    planes(left)


def per_device(queries, newest_key_value, prefix_kv, suffix_pool, page_table, suffix_pages, arrival):
    vmem = pl.BlockSpec(memory_space=pltpu.VMEM)
    smem = pl.BlockSpec(memory_space=pltpu.SMEM)
    hbm = pl.BlockSpec(memory_space=pl.ANY)
    dma = pltpu.SemaphoreType.DMA
    rows = AGENTS * ROWS
    pool = suffix_pool.reshape(suffix_pool.shape[0], suffix_pool.shape[2], suffix_pool.shape[3])
    return pl.pallas_call(
        kernel,
        out_shape=jax.ShapeDtypeStruct(queries.shape, BF16),
        in_specs=[vmem, vmem, smem, smem, smem, hbm, hbm],
        out_specs=vmem,
        scratch_shapes=[
            pltpu.VMEM((N_PRE, TOKENS, 2 * HEAD), BF16),
            pltpu.VMEM((POOL, PAGE, 2 * HEAD), BF16),
            pltpu.VMEM((AGENTS, MSG, HEAD), BF16),
            pltpu.VMEM((AGENTS, 16, HEAD), F32),
            pltpu.VMEM((N_REP, MSG, HEAD), BF16),
            pltpu.VMEM((N_REP, MSG, HEAD), BF16),
            pltpu.VMEM((8, HEAD), I32),
            pltpu.SMEM((8, HEAD), I32),
            pltpu.VMEM((AGENTS + 8, HEAD), I32),
            pltpu.SMEM((AGENTS + 8, HEAD), I32),
            pltpu.VMEM((AGENTS, ROWS, HEAD), F32),
            pltpu.VMEM((AGENTS, ROWS, HEAD), F32),
            pltpu.VMEM((N_REP, ROWS, 2 * HEAD), BF16),
            pltpu.VMEM((N_REP, ROWS, 2 * HEAD), BF16),
            pltpu.VMEM((BLOCK, TOKENS), F32),
            pltpu.VMEM((BLOCK, TOKENS), F32),
            pltpu.VMEM((BLOCK, 128), F32),
            pltpu.VMEM((BLOCK, 128), F32),
            pltpu.VMEM((rows, HEAD), F32),
            pltpu.VMEM((rows, HEAD), F32),
            pltpu.VMEM((rows, HEAD), F32),
            dma((N_PRE,)), dma((N_PRE,)),
            dma((N_PRE,)), dma((N_PRE,)),
            dma((N_PRE,)), dma((N_PRE,)),
            dma((1,)), dma((1,)),
            dma((1,)), dma((1,)),
            dma((3,)),
        ],
        compiler_params=pltpu.CompilerParams(
            collective_id=0, has_side_effects=True, vmem_limit_bytes=60 << 20),
    )(queries, newest_key_value[:, :, 0, :], arrival, page_table.T, suffix_pages, prefix_kv, pool)


def solution(mesh):
    return jax.shard_map(
        per_device,
        mesh=mesh,
        in_specs=(
            P(None, "rep", "pre", None),
            P(None, "rep", "pre", None),
            P(None, "pre", None),
            P("rep", "pre", None, None),
            P("rep", None),
            P("rep"),
            P("rep"),
        ),
        out_specs=P(None, "rep", "pre", None),
        check_vma=False,
    )
```

```python
import functools

import jax
import jax.numpy as jnp
from jax import lax
from jax.experimental import pallas as pl
from jax.experimental.pallas import tpu as pltpu
from jax.sharding import PartitionSpec as P

MESH = pl.DeviceIdType.MESH
BF16 = jnp.bfloat16
F32 = jnp.float32
I32 = jnp.int32

N_REP, N_PRE = 32, 8
X_SIZE, Y_SIZE = 4, 4
TOKENS = 2048
HALF = TOKENS // 2
QUARTER = HALF // 4
AGENTS = 32
ROWS = 32
HEAD = 128
PAGE = 128
POOL = 56
MSG = 48
BLOCK = 512
BLOCKS = AGENTS * ROWS // BLOCK
CHUNK = 256
TO_LOG2 = HEAD ** (-0.5) * 1.4426950408889634
LOW = -1e30


def kernel(
    q_ref, new_ref, arrival_ref, table_ref, pages_ref, prefix_ref, pool_hbm,
    out_ref,
    kv, pool, local, tail, asked, req_out, ask_v, ask_s, idx_v, idx_s, res, res_lse, ans_out, ans_in,
    s0, s1, m0, m1, acc, m_run, l_run,
    zs, zr, xs, xr, ss, sr, rqs, rqr, rps, rpr, loc,
):
    rep = lax.axis_index("rep")
    pre = lax.axis_index("pre")
    core = lax.rem(rep, 2)
    x = lax.rem(rep // 2, X_SIZE)
    y = rep // (2 * X_SIZE)
    sibling = rep + 1 - 2 * core

    def at_xy(xx, yy):
        return (lax.rem(yy + Y_SIZE, Y_SIZE) * X_SIZE + lax.rem(xx + X_SIZE, X_SIZE)) * 2 + core

    x_up, x_down = at_xy(x + 1, y), at_xy(x - 1, y)
    y_up, y_down = at_xy(x, y + 1), at_xy(x, y - 1)
    swap = core == 1
    a_up, a_down = jnp.where(swap, y_up, x_up), jnp.where(swap, y_down, x_down)
    b_up, b_down = jnp.where(swap, x_up, y_up), jnp.where(swap, x_down, y_down)
    mine = lax.rem(jnp.where(swap, y + 2 * x, x + 2 * y), 4)

    def spot(which, size=QUARTER, extra=0):
        start = core * HALF + lax.rem(which + 4, 4) * QUARTER + extra
        return pl.ds(pl.multiple_of(start, 128), size)

    def shard_of(k):
        k = jnp.int32(k)
        far = (k + 1) // 2
        return lax.rem(pre + jnp.where(lax.rem(k, 2) == 1, far, -far) + N_PRE, N_PRE)

    def z_send(plane):
        where = spot(mine)
        return pltpu.make_async_remote_copy(
            src_ref=prefix_ref.at[plane, where, :], dst_ref=kv.at[pre, where, :],
            send_sem=zs.at[plane], recv_sem=zr.at[pre], device_id=(rep, plane), device_id_type=MESH)

    def z_recv(p):
        where = spot(mine)
        return pltpu.make_async_remote_copy(
            src_ref=kv.at[p, where, :], dst_ref=kv.at[p, where, :],
            send_sem=zs.at[p], recv_sem=zr.at[p], device_id=(rep, p), device_id_type=MESH)

    def xy_copies(p, which, who):
        out = []
        for i, (size, extra) in enumerate(
            ((QUARTER, 0), (QUARTER, 0), (QUARTER // 2, 0), (QUARTER // 2, QUARTER // 2))
        ):
            ref = kv.at[p, spot(which[i], size, extra), :]
            out.append(pltpu.make_async_remote_copy(
                src_ref=ref, dst_ref=ref, send_sem=xs.at[p], recv_sem=xr.at[p],
                device_id=(who[i], pre), device_id_type=MESH))
        return out

    def xy_send(p):
        return xy_copies(p, (mine, mine, mine, mine), (a_up, a_down, b_up, b_down))

    def xy_all(p):
        ref = kv.at[p, pl.ds(0, 3 * QUARTER), :]
        return pltpu.make_async_remote_copy(
            src_ref=ref, dst_ref=ref, send_sem=xs.at[p], recv_sem=xr.at[p],
            device_id=(a_up, pre), device_id_type=MESH)

    def sib_copy(p, half):
        ref = kv.at[p, pl.ds(pl.multiple_of(half * HALF, HALF), HALF), :]
        return pltpu.make_async_remote_copy(
            src_ref=ref, dst_ref=ref, send_sem=ss.at[p], recv_sem=sr.at[p],
            device_id=(sibling, pre), device_id_type=MESH)

    def request(slot, other):
        return pltpu.make_async_remote_copy(
            src_ref=req_out.at[slot], dst_ref=asked.at[rep],
            send_sem=rqs.at[0], recv_sem=rqr.at[0], device_id=(other, pre), device_id_type=MESH)

    def answer(slot, other):
        return pltpu.make_async_remote_copy(
            src_ref=ans_out.at[slot], dst_ref=ans_in.at[rep],
            send_sem=rps.at[0], recv_sem=rpr.at[0], device_id=(other, pre), device_id_type=MESH)

    def all_of(buf, send, recv):
        ref = buf.at[pl.ds(0, N_REP - 1)]
        return pltpu.make_async_remote_copy(
            src_ref=ref, dst_ref=ref, send_sem=send.at[0], recv_sem=recv.at[0],
            device_id=(sibling, pre), device_id_type=MESH)

    def peers(fn):
        def one(i, c):
            fn(lax.rem(rep + i, N_REP))
            return c
        lax.fori_loop(1, N_REP, one, 0)

    def planes(fn):
        def one(k, c):
            fn(shard_of(k))
            return c
        lax.fori_loop(1, N_PRE, one, 0)

    own = pltpu.make_async_copy(prefix_ref.at[pre], kv.at[pre], loc.at[0])
    own.start()
    pool_copy = pltpu.make_async_copy(pool_hbm, pool, loc.at[1])
    pool_copy.start()
    barrier = pltpu.get_barrier_semaphore()
    peers(lambda o: pl.semaphore_signal(barrier, inc=1, device_id=(o, pre), device_id_type=MESH))
    planes(lambda p: pl.semaphore_signal(barrier, inc=1, device_id=(rep, p), device_id_type=MESH))

    lane = lax.broadcasted_iota(I32, (AGENTS, HEAD), 1)
    sub = lax.broadcasted_iota(I32, (AGENTS, HEAD), 0)
    old = jnp.zeros((AGENTS, HEAD), I32)
    for j in range(AGENTS):
        old = jnp.where(sub == j, arrival_ref[j], old)
    from_rep = lax.shift_right_logical(old, 5)
    asker = jnp.max(jnp.where(from_rep == lane, sub, 0), axis=0, keepdims=True)
    ask_v[...] = jnp.broadcast_to(asker, (8, HEAD))
    ask_put = pltpu.make_async_copy(ask_v, ask_s, loc.at[2])
    ask_put.start()

    pl.semaphore_wait(barrier, N_REP - 1 + N_PRE - 1)

    def z_sends(first, last):
        def one(k, c):
            z_send(shard_of(k)).start()
            return c
        lax.fori_loop(first, last, one, 0)
    z_sends(1, 5)

    for t in range(4):
        tail[:, t, :] = new_ref[t, :, :HEAD].astype(F32)
        tail[:, 4 + t, :] = new_ref[t, :, HEAD:].astype(F32)
    tail[:, 8, :] = (old & 31).astype(F32)
    tail[:, 9, :] = from_rep.astype(F32)
    for t in range(10, 16):
        tail[:, t, :] = jnp.zeros((AGENTS, HEAD), F32)

    def build(i, c):
        for u in range(8):
            j = i * 8 + u
            rows = jnp.concatenate([q_ref[t, j].astype(F32) for t in range(4)] + [tail[j]], axis=0)
            local[j] = rows.astype(BF16)
        return c
    lax.fori_loop(0, AGENTS // 8, build, 0)

    ask_put.wait()

    def ask(o):
        req_out[o] = local[ask_s[0, o]]
        request(o, o).start()
    peers(ask)
    asked[rep] = jnp.zeros((MSG, HEAD), BF16)
    ans_in[rep] = jnp.zeros((ROWS, 2 * HEAD), BF16)

    m_run[...] = jnp.full_like(m_run, LOW)
    l_run[...] = jnp.zeros_like(l_run)
    acc[...] = jnp.zeros_like(acc)
    score_bufs, peak_bufs = (s0, s1), (m0, m1)
    per = BLOCK // ROWS

    def block_queries(b):
        return local[b * per:(b + 1) * per, :ROWS, :].reshape(BLOCK, HEAD)

    def score_chunk(q, p, u, kc, peak):
        k = kv[p, kc * CHUNK:(kc + 1) * CHUNK, :HEAD]
        s = lax.dot_general(q, k, (((1,), (1,)), ((), ())), preferred_element_type=F32)
        score_bufs[u][:, kc * CHUNK:(kc + 1) * CHUNK] = s
        for j in range(CHUNK // 128):
            part = s[:, j * 128:(j + 1) * 128]
            peak = part if peak is None else jnp.maximum(peak, part)
        return peak

    def keep_peak(u, peak):
        peak_bufs[u][...] = jnp.broadcast_to(jnp.max(peak, axis=1, keepdims=True), (BLOCK, 128))

    ones = jnp.ones((CHUNK, HEAD), BF16)

    def step(b, p, b_next, p_next, beside=None):
        u = b % 2
        if b_next is not None:
            v = b_next % 2
            q = block_queries(b_next)
        peak = peak_bufs[u][:, :1]
        nxt = None
        out = None

        def values(kc, w):
            both = jnp.concatenate([kv[p, kc * CHUNK:(kc + 1) * CHUNK, HEAD:], ones], axis=1)
            d = jnp.dot(w, both, preferred_element_type=F32)
            return d if out is None else out + d

        last = None
        for kc in range(TOKENS // CHUNK):
            w = jnp.exp2((score_bufs[u][:, kc * CHUNK:(kc + 1) * CHUNK] - peak) * TO_LOG2).astype(BF16)
            if b_next is not None:
                nxt = score_chunk(q, p_next, v, kc, nxt)
            if last is not None:
                out = values(kc - 1, last)
            last = w
            if beside is not None:
                beside(kc)
        out = values(TOKENS // CHUNK - 1, last)
        if b_next is not None:
            keep_peak(v, nxt)
        rows = slice(b * BLOCK, (b + 1) * BLOCK)
        top = peak_bufs[u][...] * TO_LOG2
        old = m_run[rows, :]
        new = jnp.maximum(old, top)
        f_old, f_new = jnp.exp2(old - new), jnp.exp2(top - new)
        m_run[rows, :] = new
        l_run[rows, :] = l_run[rows, :] * f_old + out[:, HEAD:] * f_new
        acc[rows, :] = acc[rows, :] * f_old + out[:, :HEAD] * f_new

    def place_agents():
        all_of(asked, rqs, rqr).wait_recv()
        told = asked[:, ROWS:, :].astype(F32)
        slots = told[:, 8, :].astype(I32)
        reps = told[:, 9, :].astype(I32)
        for_me = (reps == rep) & (sub != rep)
        moved = jnp.where(for_me & (slots == lane), sub, 0)
        stays = jnp.where((from_rep == rep) & ((old & 31) == lane), sub + AGENTS, 0)
        at = jnp.max(jnp.maximum(moved, stays), axis=0, keepdims=True)
        idx_v[:AGENTS, :] = jnp.where(for_me, slots & 31, 0)
        idx_v[AGENTS:, :] = jnp.broadcast_to(at, (8, HEAD))
        put = pltpu.make_async_copy(idx_v, idx_s, loc.at[2])
        put.start()
        put.wait()

    dims = (((1,), (1,)), ((), ()))
    lanes_n = lax.broadcasted_iota(I32, (ROWS, 8), 1)
    steps_n = lax.shift_right_logical(lax.broadcasted_iota(I32, (ROWS, 8), 0), 3)
    lanes_p = lax.broadcasted_iota(I32, (ROWS, 2 * PAGE), 1)

    def suffix_some(agents):
        scored = []
        for a in agents:
            at = idx_s[AGENTS, a]
            msg = jnp.where(at >= AGENTS, local[at & 31], asked[at & 31])
            new = msg[ROWS:].astype(F32)[:8]
            page0, page1 = table_ref[0, a], table_ref[1, a]
            keys = jnp.concatenate([pool[page0, :, :HEAD], pool[page1, :, :HEAD]], axis=0)
            q = msg[:ROWS]
            c = lax.dot_general(q, keys, dims, preferred_element_type=F32)
            cn = lax.dot_general(q, new.astype(BF16), dims, preferred_element_type=F32)
            scored.append((a, page0, page1, new, c, cn))
        weighed = []
        for a, page0, page1, new, c, cn in scored:
            c = jnp.where(lanes_p < pages_ref[a] * PAGE, c, LOW)
            cn = jnp.where(lanes_n <= steps_n, cn, LOW)
            peak = jnp.maximum(jnp.max(c, axis=1, keepdims=True), jnp.max(cn, axis=1, keepdims=True))
            w = jnp.exp2((c - peak) * TO_LOG2)
            wn = jnp.exp2((cn - peak) * TO_LOG2)
            total = jnp.sum(w, axis=1, keepdims=True) + jnp.sum(wn, axis=1, keepdims=True)
            weighed.append((a, page0, page1, new, peak, w.astype(BF16), wn.astype(BF16), total))
        outs = []
        for a, page0, page1, new, peak, w, wn, total in weighed:
            values = jnp.concatenate([pool[page0, :, HEAD:], pool[page1, :, HEAD:]], axis=0)
            newest = jnp.concatenate([new[4:], new[:4]], axis=0).astype(BF16)
            o = jnp.dot(w, values, preferred_element_type=F32)
            o = o + jnp.dot(wn, newest, preferred_element_type=F32)
            outs.append((a, o / total, jnp.broadcast_to(peak * TO_LOG2 + jnp.log2(total), (ROWS, HEAD))))
        for a, o, lse in outs:
            res[a] = o
            res_lse[a] = lse

    def suffix_range(first, last):
        def some(i, c):
            suffix_some([i * 8 + j for j in range(8)])
            return c
        lax.fori_loop(first // 8, last // 8, some, 0)

    answer_lanes = lax.broadcasted_iota(I32, (ROWS, HEAD), 1)

    def send_answer(i):
        o = lax.rem(rep + i, N_REP)
        a = idx_s[o, 0]
        ans_out[o, :, :HEAD] = res[a].astype(BF16)
        lse = res_lse[a]
        hi = lse.astype(BF16).astype(F32)
        mid = (lse - hi).astype(BF16).astype(F32)
        low = lse - hi - mid
        ans_out[o, :, HEAD:] = jnp.where(
            answer_lanes < 32, hi, jnp.where(answer_lanes < 64, mid, low)).astype(BF16)
        answer(o, o).start()

    def forward_z(p):
        z_recv(p).wait_recv()
        for c in xy_send(p):
            c.start()

    def forward_xy(p):
        xy_all(p).wait_recv()
        sib_copy(p, core).start()

    own.wait()
    peak = None
    q_first = block_queries(0)
    for kc in range(TOKENS // CHUNK):
        peak = score_chunk(q_first, pre, 0, kc, peak)
    keep_peak(0, peak)

    def next_arrived(p):
        sib_copy(p, 1 - core).wait_recv()

    first, second = shard_of(1), shard_of(2)
    forward_z(first)
    forward_z(second)
    z_sends(5, N_PRE)
    step(0, pre, 1, pre)
    pool_copy.wait()
    place_agents()
    forward_z(shard_of(3))
    forward_z(shard_of(4))
    forward_xy(first)
    suffix_range(0, 16)
    forward_xy(second)
    suffix_range(16, 32)
    def all_answers(i, c):
        send_answer(i)
        return c
    lax.fori_loop(1, N_REP, all_answers, 0)
    next_arrived(first)
    step(1, pre, 0, first)

    passed = {
        (1, 0): (forward_xy, 3), (1, 1): (forward_xy, 4),
        (2, 0): (forward_z, 5), (2, 1): (forward_z, 6),
        (3, 1): (forward_xy, 5), (4, 0): (forward_z, 7),
        (4, 1): (forward_xy, 6), (5, 1): (forward_xy, 7),
    }

    def shard(k, c):
        p = shard_of(k)
        p_next = shard_of(k + 1)
        for b in range(BLOCKS):
            for (at, ahead_of), (pass_on, which) in passed.items():
                if ahead_of == b:
                    pl.when(k == at)(functools.partial(pass_on, shard_of(which)))
            if b == BLOCKS - 1:
                next_arrived(p_next)
                step(b, p, 0, p_next)
            else:
                step(b, p, b + 1, p)
        return c

    lax.fori_loop(1, N_PRE - 1, shard, 0)

    def finish(j):
        old = arrival_ref[j]
        src = lax.shift_right_logical(old, 5)
        slot = lax.rem(old, AGENTS)
        got = ans_in[src].astype(F32)
        stays = src == rep
        part = jnp.where(stays, res[slot], got[:, :HEAD])
        lse_got = got[:, HEAD:HEAD + 1] + got[:, HEAD + 32:HEAD + 33] + got[:, HEAD + 64:HEAD + 65]
        lse = jnp.where(stays, res_lse[slot], lse_got)
        rows = slice(j * ROWS, (j + 1) * ROWS)
        m = m_run[rows, :]
        top = jnp.maximum(m, lse)
        f, g = jnp.exp2(m - top), jnp.exp2(lse - top)
        o = (acc[rows, :] * f + part * g) / (l_run[rows, :] * f + g)
        for t in range(4):
            out_ref[t, j] = o[t * 8:(t + 1) * 8].astype(BF16)

    last_shard = shard_of(N_PRE - 1)
    step(0, last_shard, 1, last_shard)
    all_of(ans_in, rps, rpr).wait_recv()
    each = AGENTS // BLOCKS // (TOKENS // CHUNK)

    def finish_some(kc):
        for j in range(kc * each, (kc + 1) * each):
            finish(j)

    step(1, last_shard, None, None, finish_some)
    for j in range(AGENTS // BLOCKS, AGENTS):
        finish(j)

    all_of(req_out, rqs, rqr).wait_send()
    all_of(ans_out, rps, rpr).wait_send()

    def left(p):
        z_send(p).wait_send()
        xy_all(p).wait_send()
        sib_copy(p, core).wait_send()
    planes(left)


def per_device(queries, newest_key_value, prefix_kv, suffix_pool, page_table, suffix_pages, arrival):
    vmem = pl.BlockSpec(memory_space=pltpu.VMEM)
    smem = pl.BlockSpec(memory_space=pltpu.SMEM)
    hbm = pl.BlockSpec(memory_space=pl.ANY)
    dma = pltpu.SemaphoreType.DMA
    rows = AGENTS * ROWS
    pool = suffix_pool.reshape(suffix_pool.shape[0], suffix_pool.shape[2], suffix_pool.shape[3])
    return pl.pallas_call(
        kernel,
        out_shape=jax.ShapeDtypeStruct(queries.shape, BF16),
        in_specs=[vmem, vmem, smem, smem, smem, hbm, hbm],
        out_specs=vmem,
        scratch_shapes=[
            pltpu.VMEM((N_PRE, TOKENS, 2 * HEAD), BF16),
            pltpu.VMEM((POOL, PAGE, 2 * HEAD), BF16),
            pltpu.VMEM((AGENTS, MSG, HEAD), BF16),
            pltpu.VMEM((AGENTS, 16, HEAD), F32),
            pltpu.VMEM((N_REP, MSG, HEAD), BF16),
            pltpu.VMEM((N_REP, MSG, HEAD), BF16),
            pltpu.VMEM((8, HEAD), I32),
            pltpu.SMEM((8, HEAD), I32),
            pltpu.VMEM((AGENTS + 8, HEAD), I32),
            pltpu.SMEM((AGENTS + 8, HEAD), I32),
            pltpu.VMEM((AGENTS, ROWS, HEAD), F32),
            pltpu.VMEM((AGENTS, ROWS, HEAD), F32),
            pltpu.VMEM((N_REP, ROWS, 2 * HEAD), BF16),
            pltpu.VMEM((N_REP, ROWS, 2 * HEAD), BF16),
            pltpu.VMEM((BLOCK, TOKENS), F32),
            pltpu.VMEM((BLOCK, TOKENS), F32),
            pltpu.VMEM((BLOCK, 128), F32),
            pltpu.VMEM((BLOCK, 128), F32),
            pltpu.VMEM((rows, HEAD), F32),
            pltpu.VMEM((rows, HEAD), F32),
            pltpu.VMEM((rows, HEAD), F32),
            dma((N_PRE,)), dma((N_PRE,)),
            dma((N_PRE,)), dma((N_PRE,)),
            dma((N_PRE,)), dma((N_PRE,)),
            dma((1,)), dma((1,)),
            dma((1,)), dma((1,)),
            dma((3,)),
        ],
        compiler_params=pltpu.CompilerParams(
            collective_id=0, has_side_effects=True, vmem_limit_bytes=60 << 20),
    )(queries, newest_key_value[:, :, 0, :], arrival, page_table.T, suffix_pages, prefix_kv, pool)


def solution(mesh):
    return jax.shard_map(
        per_device,
        mesh=mesh,
        in_specs=(
            P(None, "rep", "pre", None),
            P(None, "rep", "pre", None),
            P(None, "pre", None),
            P("rep", "pre", None, None),
            P("rep", None),
            P("rep"),
            P("rep"),
        ),
        out_specs=P(None, "rep", "pre", None),
        check_vma=False,
    )
```
